512 devices in a mesh: ctx: 64 (over y, z_lo, core), head: 8 (over x, z_hi).
Axes of the slice: x: 4, y: 8, z: 8 (z_hi: 2, z_lo: 4; z = z_hi * 4 + z_lo), core: 2. Of those that a mesh axis runs over, the one named last changes fastest.
Arguments:
- index_query: bfloat16 [8192, 4096], P(('ctx', 'head')), may hold values from -6 to 6
- index_weight: float32 [8192, 32], P(('ctx', 'head')), may hold values from -1 to 1
- index_key: bfloat16 [8192, 128], P('ctx'), may hold values from -6 to 6
- latent_query: bfloat16 [8192, 36864], P('ctx', 'head'), may hold values from -20 to 20
- latent: bfloat16 [8192, 576], P('ctx'), may hold values from -6 to 6
- block_lists: int32 [64, 16], P('ctx'), may hold values from -1 to 63, as said below
- value_up: bfloat16 [64, 512, 128], P('head'), may hold values from -0.25 to 0.25
- out_weight: bfloat16 [8192, 3584], P('head', 'ctx'), may hold values from -0.1875 to 0.1875
Outputs:
- index_scores: float32 [8192, 8192], P(('ctx', 'head'))
- attn_out: bfloat16 [8192, 3584], P('ctx', 'head')
The draws below stay inside these ranges and needn't reach their ends.
Inputs may be any that keep to these rules, and one draw needn't show every extreme that they name: `block_lists`: row b lists b itself first, then min(15, b) distinct blocks below b; the remaining entries are -1.
All inputs are finite; a program needn't handle non-finite values.
Results may differ from the reference program's by a relative error of at most 0.02.
Values may be sent and summed in bfloat16 or wider, within the bound.
No kernel may reach another device: no remote copies, remote signals or barrier semaphores. Data moves between devices by JAX's collectives and lax.ppermute only.
A program may use at most 64 MiB of HBM per device.

```python
import jax
import jax.numpy as jnp
from jax import lax

TOK_DEV = 128
HEADS = 64
KV_RANK = 512
ROPE_DIM = 64
V_DIM = 128
IDX_HEADS = 32
IDX_DIM = 128
D_OUT = 3584
BLOCK = 128
TOPK = 16
TOKENS = 8192
NBLK = 64
N_CTX = 64


def latent_base(key):
    lat_width = KV_RANK + ROPE_DIM
    normal_part = jax.random.normal(key, (TOKENS, lat_width), jnp.float32)
    return normal_part


def draw_latent(key, part):
    normal_part = latent_base(key)
    values = jnp.clip(normal_part, -6.0, 6.0)
    return values.astype(jnp.bfloat16)


def draw_latent_query(key, part):
    key = jax.random.fold_in(key, 7)
    lat_width = KV_RANK + ROPE_DIM
    values = jnp.clip(jax.random.normal(key, (TOKENS, HEADS, lat_width), jnp.float32), -6.0, 6.0)
    return values.reshape(TOKENS, HEADS * lat_width).astype(jnp.bfloat16)


def draw_block_lists(key, part):
    key = jax.random.fold_in(key, 11)
    row_keys = jax.random.split(key, NBLK)

    def one_order(row_key):
        return jax.random.permutation(row_key, NBLK).astype(jnp.int32)
    orders = jax.vmap(one_order)(row_keys)
    candidate = jnp.arange(NBLK, dtype=jnp.int32)[None, :]
    owner = jnp.arange(NBLK, dtype=jnp.int32)[:, None]
    earlier = candidate < owner
    favoured = ((candidate == 0) | (candidate == owner - 1)).astype(jnp.int32)
    ranking = orders + 2 * NBLK * favoured
    ranking = jnp.where(earlier, ranking, orders - 4 * NBLK)
    top_values, top_index = lax.top_k(ranking, TOPK - 1)
    listed = jnp.where(top_values >= 0, top_index.astype(jnp.int32), -1)
    return jnp.concatenate([owner, listed], axis=1).astype(jnp.int32)


def with_spikes(entries, key, source, target, blocks, factor):
    owner, partner = [(jnp.arange(entries.shape[axis_at]) // (entries.shape[axis_at] // blocks)).reshape([-1 if axis == axis_at else 1 for axis in range(entries.ndim)]) for axis_at in (source, target)]
    chosen = jax.random.permutation(key, blocks)[partner]
    strong = (owner == chosen) | (owner == (partner + blocks // 2) % blocks)
    return jnp.where(strong, factor * entries, entries)


def steps_of(rng, shape, cuts, low, high):
    def one(dim, parts):
        heights = jax.random.uniform(jax.random.fold_in(jax.random.fold_in(rng, 6), dim), (parts,), jnp.float32, low / len(cuts), high / len(cuts))
        return jnp.repeat(jnp.exp(heights), shape[dim] // parts).reshape((-1,) + (1,) * (len(shape) - dim - 1))

    loudness = one(*cuts[0])
    for cut in cuts[1:]:
        loudness = loudness * one(*cut)
    return loudness


def centred(key, extent, scale, reach, shards=(), kind=jnp.bfloat16):
    factor_of = steps_of(key, extent, shards, -0.22, 0.18) if shards else 1.0
    array = jax.random.normal(key, extent, jnp.float32) * scale * factor_of
    return jnp.minimum(jnp.maximum(array, -reach), reach).astype(kind)


def heavy_noise(own_key, dims, spread, most, cuts, heavy, held_as=jnp.bfloat16):
    result = spread * jax.random.normal(own_key, dims, jnp.float32)
    if cuts:
        result = result * steps_of(own_key, dims, cuts, -0.22, 0.18)
    return jnp.clip(with_spikes(result, jax.random.fold_in(own_key, 3), *heavy), -most, most).astype(held_as)


def setup_inputs(seed: int = 0) -> dict:
    streams_of = jax.random.split(jax.random.key(seed), 9)
    index_query = centred(streams_of[0], (TOKENS, IDX_HEADS * IDX_DIM), 1.0, 6.0, ((0, 512),))
    index_weight = centred(streams_of[1], (TOKENS, IDX_HEADS), IDX_HEADS ** -0.5, 1.0, ((0, 512),), jnp.float32)
    index_key = centred(streams_of[2], (TOKENS, IDX_DIM), 1.0, 6.0, ((0, 64),))
    latent_query = draw_latent_query(jax.random.fold_in(streams_of[8], 71), 0)
    latent = draw_latent(jax.random.fold_in(streams_of[8], 71), 0)
    block_lists = draw_block_lists(jax.random.fold_in(streams_of[8], 71), 0)
    value_up = centred(streams_of[6], (HEADS, KV_RANK, V_DIM), KV_RANK ** -0.5, 0.25, ((0, 8),))
    out_weight = heavy_noise(streams_of[7], (HEADS * V_DIM, D_OUT), (HEADS * V_DIM) ** -0.5, 0.1875, ((0, 8), (1, 64)), (0, 1, 64, 4.0))
    return {"index_query": index_query, "index_weight": index_weight, "index_key": index_key, "latent_query": latent_query, "latent": latent, "block_lists": block_lists, "value_up": value_up, "out_weight": out_weight}


attention_scale = 192.0 ** -0.5
masked_value = -1.0e30


def reference(index_query, index_weight, index_key, latent_query, latent, block_lists, value_up, out_weight):
    lat_width = KV_RANK + ROPE_DIM

    def index_rows(shard_number):
        first_row = shard_number * TOK_DEV
        query_rows = lax.dynamic_slice_in_dim(index_query, first_row, TOK_DEV, 0).reshape(TOK_DEV * IDX_HEADS, IDX_DIM)
        head_weight = lax.dynamic_slice_in_dim(index_weight, first_row, TOK_DEV, 0)
        raw_dots = lax.dot_general(query_rows, index_key, (((1,), (1,)), ((), ())), preferred_element_type=jnp.float32)
        active = jnp.maximum(raw_dots * (IDX_DIM ** -0.5), 0.0).reshape(TOK_DEV, IDX_HEADS, TOKENS)
        summed = jnp.einsum("thk,th->tk", active, head_weight.astype(jnp.float32))
        row_pos = first_row + jnp.arange(TOK_DEV, dtype=jnp.int32)
        key_pos = jnp.arange(TOKENS, dtype=jnp.int32)
        return jnp.where(key_pos[None, :] <= row_pos[:, None], summed, jnp.zeros_like(summed))

    index_scores = lax.map(index_rows, jnp.arange(N_CTX, dtype=jnp.int32)).reshape(TOKENS, TOKENS)

    block_pool = latent.reshape(NBLK, BLOCK, lat_width)

    def attend_tile(tile_number):
        listed = block_lists[tile_number]
        safe_list = jnp.maximum(listed, 0).astype(jnp.int32)
        pulled = jnp.take(block_pool, safe_list, axis=0).reshape(TOPK * BLOCK, lat_width)
        key_pos = (safe_list[:, None] * BLOCK + jnp.arange(BLOCK, dtype=jnp.int32)[None, :]).reshape(TOPK * BLOCK)
        key_live = jnp.repeat(listed >= 0, BLOCK)
        query_pos = tile_number * BLOCK + jnp.arange(BLOCK, dtype=jnp.int32)
        allowed = key_live[None, :] & (key_pos[None, :] <= query_pos[:, None])
        tile_query = lax.dynamic_slice_in_dim(latent_query, tile_number * BLOCK, BLOCK, 0).reshape(BLOCK, HEADS, lat_width)
        scores = jnp.einsum("qhc,kc->hqk", tile_query.astype(jnp.float32), pulled.astype(jnp.float32)) * attention_scale
        scores = jnp.where(allowed[None], scores, masked_value)
        row_max = jnp.max(scores, axis=-1, keepdims=True)
        expo_terms = jnp.where(allowed[None], jnp.exp(scores - row_max), 0.0)
        probabilities = (expo_terms / jnp.sum(expo_terms, axis=-1, keepdims=True)).astype(jnp.bfloat16)
        latent_out = jnp.einsum("hqk,kc->hqc", probabilities.astype(jnp.float32), pulled[:, :KV_RANK].astype(jnp.float32)).astype(jnp.bfloat16)
        head_values = jnp.einsum("hqc,hcv->qhv", latent_out.astype(jnp.float32), value_up.astype(jnp.float32)).astype(jnp.bfloat16)
        flat_values = head_values.reshape(BLOCK, HEADS * V_DIM)
        return jnp.dot(flat_values, out_weight, preferred_element_type=jnp.float32).astype(jnp.bfloat16)

    attn_out = lax.map(attend_tile, jnp.arange(NBLK, dtype=jnp.int32)).reshape(TOKENS, D_OUT)
    return index_scores, attn_out
```

```python
import jax
import jax.numpy as jnp
from jax import lax
from jax.experimental import pallas as pl
from jax.experimental.pallas import tpu as pltpu
from jax.sharding import Mesh
from jax.sharding import PartitionSpec as P

TOK_DEV = 128
HEADS_DEV = 8
KV_RANK = 512
LAT = 576
V_DIM = 128
IDX_HEADS = 32
IDX_DIM = 128
BLOCK = 128
TOPK = 16
NBLK = 64
COLS = 56
NY, NZ, NC, NX, NW = 8, 4, 2, 4, 2

CTX = ("y", "z", "c")
HEAD = ("x", "w")
LOG2E = 1.4426950408889634
SCORE_SCALE = 192.0 ** (-0.5) * LOG2E
MASKED = -1e30
VMEM_LIMIT = 56 * 1024 * 1024


def attend_kernel(q_ref, kv_ref, bias_ref, up_ref, out_ref, vt_ref):
    vt_ref[...] = kv_ref[:, :KV_RANK].T
    bias = bias_ref[...]
    bias2 = jnp.concatenate([bias, bias], axis=1)
    for pair in range(HEADS_DEV // 2):
        scores = lax.dot_general(
            kv_ref[...], q_ref[pair], (((1,), (1,)), ((), ())), preferred_element_type=jnp.float32
        )
        scores = scores + bias2
        row_max = jnp.max(scores, axis=0, keepdims=True)
        expo = jnp.exp2((scores - row_max) * SCORE_SCALE)
        total = jnp.sum(expo, axis=0, keepdims=True)
        lat_out = lax.dot_general(
            vt_ref[...],
            expo.astype(jnp.bfloat16),
            (((1,), (0,)), ((), ())),
            preferred_element_type=jnp.float32,
        )
        lat_out = (lat_out / total).astype(jnp.bfloat16)
        for half in range(2):
            head = 2 * pair + half
            values = lax.dot_general(
                up_ref[head],
                lat_out[:, half * BLOCK : (half + 1) * BLOCK],
                (((1,), (0,)), ((), ())),
                preferred_element_type=jnp.float32,
            )
            out_ref[head * V_DIM : (head + 1) * V_DIM, :] = values.astype(jnp.bfloat16)


def attend(queries, kv, bias, up_t):
    return pl.pallas_call(
        attend_kernel,
        out_shape=jax.ShapeDtypeStruct((HEADS_DEV * V_DIM, BLOCK), jnp.bfloat16),
        in_specs=[pl.BlockSpec(memory_space=pltpu.VMEM)] * 4,
        out_specs=pl.BlockSpec(memory_space=pltpu.VMEM),
        scratch_shapes=[pltpu.VMEM((KV_RANK, TOPK * BLOCK), jnp.bfloat16)],
        compiler_params=pltpu.CompilerParams(vmem_limit_bytes=VMEM_LIMIT),
        name="attend",
    )(queries, kv, bias, up_t)


def index_kernel(place_ref, q_ref, w_ref, own_ref, other_ref, out_ref, wb_ref):
    core = place_ref[0]
    first_row = place_ref[1]
    rows = 16
    for head in range(IDX_HEADS):
        wb_ref[head * rows : (head + 1) * rows, :] = jnp.broadcast_to(
            w_ref[:, head : head + 1] * (IDX_DIM ** (-0.5)), (rows, BLOCK)
        )
    row_pos = first_row + lax.broadcasted_iota(jnp.int32, (rows, BLOCK), 0)
    lane = lax.broadcasted_iota(jnp.int32, (rows, BLOCK), 1)

    def chunk(keys_ref, parity, step):
        keys = keys_ref[pl.ds(step * 2, 2)].reshape(2 * BLOCK, IDX_DIM)
        dots = lax.dot_general(
            q_ref[...], keys, (((1,), (1,)), ((), ())), preferred_element_type=jnp.float32
        )
        for half in range(2):
            part = dots[:, half * BLOCK : (half + 1) * BLOCK]
            active = jnp.maximum(part, 0.0) * wb_ref[...]
            summed = jnp.sum(active.reshape(IDX_HEADS, rows, BLOCK), axis=0)
            start = pl.multiple_of(((step * 2 + half) * 2 + parity) * BLOCK, BLOCK)
            out_ref[:, pl.ds(start, BLOCK)] = jnp.where(start + lane <= row_pos, summed, 0.0)

    def one(step, carry):
        chunk(own_ref, core, step)
        chunk(other_ref, 1 - core, step)
        return carry

    lax.fori_loop(0, NBLK // 4, one, 0)


def index_part(place, query, weight, own, other):
    return pl.pallas_call(
        index_kernel,
        out_shape=jax.ShapeDtypeStruct((16, NBLK * BLOCK), jnp.float32),
        in_specs=[pl.BlockSpec(memory_space=pltpu.SMEM)]
        + [pl.BlockSpec(memory_space=pltpu.VMEM)] * 4,
        out_specs=pl.BlockSpec(memory_space=pltpu.VMEM),
        scratch_shapes=[pltpu.VMEM((IDX_HEADS * 16, BLOCK), jnp.float32)],
        compiler_params=pltpu.CompilerParams(vmem_limit_bytes=VMEM_LIMIT),
        name="index_scores",
    )(place, query, weight, own, other)


def swap_core(value):
    return lax.ppermute(value, "c", [(0, 1), (1, 0)])


def spread(value, axis, count):
    wide = jnp.broadcast_to(value[None], (count,) + value.shape)
    return lax.all_to_all(wide, axis, 0, 0)


def body(
    index_query, index_weight, index_key, latent_query, latent, block_lists, value_up, out_weight
):
    y, z, core, x, w = (lax.axis_index(name) for name in ("y", "z", "c", "x", "w"))
    ctx_pos = (y * NZ + z) * NC + core
    head_pos = x * NW + w

    own = lax.dynamic_slice_in_dim(latent, x * 32, 32, 0).reshape(1, NC, 16, LAT)
    wide = jnp.broadcast_to(own, (NY * NZ, NC, 16, LAT)).reshape(NBLK, 16, LAT)
    pool = lax.all_to_all(wide, CTX, 0, 0)

    w_t = out_weight.T
    packed = jnp.concatenate([w_t, index_key.reshape(16, 1024)], axis=0)
    packed = spread(packed, "z", NZ)
    w_all = lax.all_gather(packed[:, :COLS], "y", axis=0, tiled=True)
    w_all = w_all.reshape(NY * NZ * COLS, 1024)
    keys_z = packed[:, COLS:].reshape(NZ, BLOCK, IDX_DIM)
    keys_own = lax.all_gather(keys_z, "y", axis=0, tiled=True)
    keys_other = swap_core(keys_own)

    listed = block_lists[0]
    safe = jnp.maximum(listed, 0)
    both = jnp.concatenate([safe, swap_core(safe)])
    picked = jnp.take(pool, both, axis=0, mode="clip").reshape(2, TOPK * 16, LAT)
    mine = jnp.concatenate([picked[0], swap_core(picked[1])], axis=0)
    kv = spread(mine, "x", NX).reshape(TOPK * BLOCK, LAT)

    place = jnp.arange(TOPK * BLOCK, dtype=jnp.int32)
    from_x = place // 512
    from_core = jnp.where((place // 256) % 2 == 0, core, 1 - core)
    slot = (place // 16) % TOPK
    key_pos = safe[slot] * BLOCK + from_x * 32 + from_core * 16 + place % 16
    live = listed[slot] >= 0
    query_pos = ctx_pos * BLOCK + jnp.arange(BLOCK, dtype=jnp.int32)
    allowed = live[:, None] & (key_pos[:, None] <= query_pos[None, :])
    bias = jnp.where(allowed, 0.0, MASKED).astype(jnp.float32)

    queries = jnp.moveaxis(latent_query.reshape(BLOCK, HEADS_DEV, LAT), 1, 0)
    queries = queries.reshape(HEADS_DEV // 2, 2 * BLOCK, LAT)
    up_t = jnp.swapaxes(value_up, 1, 2)
    values = attend(queries, kv, bias, up_t)

    both_values = jnp.concatenate([values, swap_core(values)], axis=1)
    terms = jnp.dot(w_all, both_values, preferred_element_type=jnp.float32).astype(jnp.bfloat16)
    terms = terms.reshape(NY, NZ * COLS, 2 * BLOCK)
    shares = lax.all_to_all(terms, HEAD, 0, 0)
    summed = jnp.sum(shares.astype(jnp.float32), axis=0).astype(jnp.bfloat16)
    kept = summed[:, :BLOCK].reshape(NZ, COLS, BLOCK)
    other = swap_core(summed[:, BLOCK:]).reshape(NZ, COLS, BLOCK)
    first = jnp.where(core == 0, kept, other)
    second = jnp.where(core == 0, other, kept)
    attn_out = jnp.stack([first, second], axis=1).reshape(NZ * NC * COLS, BLOCK).T

    idx_query = jnp.moveaxis(index_query.reshape(16, IDX_HEADS, IDX_DIM), 1, 0)
    idx_query = idx_query.reshape(IDX_HEADS * 16, IDX_DIM)
    first_row = ctx_pos * TOK_DEV + head_pos * 16
    index_scores = index_part(
        jnp.stack([core, first_row]), idx_query, index_weight, keys_own, keys_other
    )
    return index_scores, attn_out


def solution(mesh):
    fine = Mesh(mesh.devices.reshape(NY, NZ, NC, NX, NW), ("y", "z", "c", "x", "w"))
    return jax.shard_map(
        body,
        mesh=fine,
        in_specs=(
            P(CTX + HEAD, None),
            P(CTX + HEAD, None),
            P(CTX, None),
            P(CTX, HEAD),
            P(CTX, None),
            P(CTX, None),
            P(HEAD, None, None),
            P(HEAD, CTX),
        ),
        out_specs=(P(CTX + HEAD, None), P(CTX, HEAD)),
        check_vma=False,
    )
```

```python
import functools

import jax
import jax.numpy as jnp
from jax import lax
from jax.experimental import pallas as pl
from jax.experimental.pallas import tpu as pltpu
from jax.sharding import Mesh
from jax.sharding import PartitionSpec as P

TOK_DEV = 128
HEADS_DEV = 8
KV_RANK = 512
LAT = 576
V_DIM = 128
IDX_HEADS = 32
IDX_DIM = 128
BLOCK = 128
TOPK = 16
NBLK = 64
COLS = 56
NY, NZ, NC, NX, NW = 8, 4, 2, 4, 2

CTX = ("y", "z", "c")
HEAD = ("x", "w")
LOG2E = 1.4426950408889634
SCORE_SCALE = 192.0 ** (-0.5) * LOG2E
MASKED = -1e30
VMEM_LIMIT = 56 * 1024 * 1024


def attend_kernel(count, first, last, *refs):
    place_ref, q_ref = refs[:2]
    kv_refs = refs[2 : 2 + count]
    refs = refs[2 + count :]
    if not first:
        max_in, total_in, sum_in = refs[:3]
        refs = refs[3:]
    if last:
        up_ref, out_ref = refs[:2]
        refs = refs[2:]
    else:
        max_out, total_out, sum_out = refs[:3]
        refs = refs[3:]
    bias_ref, vt_ref = refs
    keys = jnp.concatenate([ref[...] for ref in kv_refs], axis=0)
    n_keys = keys.shape[0]
    vt_ref[...] = keys[:, :KV_RANK].T
    row = lax.broadcasted_iota(jnp.int32, (16, BLOCK), 0)
    query = place_ref[TOPK] + lax.broadcasted_iota(jnp.int32, (16, BLOCK), 1)
    for group in range(n_keys // 16):
        part, slot = divmod(group, TOPK)
        entry = place_ref[slot]
        start = jnp.where(entry < 0, 2 * NBLK, entry) * BLOCK + place_ref[TOPK + 1 + part]
        seen = jnp.where(start + row <= query, 0.0, MASKED)
        bias_ref[group * 16 : (group + 1) * 16, :BLOCK] = seen
        bias_ref[group * 16 : (group + 1) * 16, BLOCK:] = seen
    for pair in range(HEADS_DEV // 2):
        scores = lax.dot_general(
            keys, q_ref[pair], (((1,), (1,)), ((), ())), preferred_element_type=jnp.float32
        )
        scores = scores + bias_ref[...]
        row_max = jnp.max(scores, axis=0, keepdims=True)
        if not first:
            row_max = jnp.maximum(row_max, max_in[pair])
            keep = jnp.exp2((max_in[pair] - row_max) * SCORE_SCALE)
        expo = jnp.exp2((scores - row_max) * SCORE_SCALE)
        total = jnp.sum(expo, axis=0, keepdims=True)
        lat_sum = lax.dot_general(
            vt_ref[...],
            expo.astype(jnp.bfloat16),
            (((1,), (0,)), ((), ())),
            preferred_element_type=jnp.float32,
        )
        if not first:
            total = total + total_in[pair] * keep
            lat_sum = lat_sum + sum_in[pair] * keep
        if not last:
            max_out[pair] = row_max
            total_out[pair] = total
            sum_out[pair] = lat_sum
            continue
        lat_out = (lat_sum / total).astype(jnp.bfloat16)
        for half in range(2):
            head = 2 * pair + half
            values = lax.dot_general(
                up_ref[head],
                lat_out[:, half * BLOCK : (half + 1) * BLOCK],
                (((1,), (0,)), ((), ())),
                preferred_element_type=jnp.float32,
            )
            out_ref[head * V_DIM : (head + 1) * V_DIM, :] = values.astype(jnp.bfloat16)


def attend(place, queries, parts, state, up_t):
    pairs = HEADS_DEV // 2
    n_keys = sum(part.shape[0] for part in parts)
    stat = jax.ShapeDtypeStruct((pairs, 1, 2 * BLOCK), jnp.float32)
    out = (stat, stat, jax.ShapeDtypeStruct((pairs, KV_RANK, 2 * BLOCK), jnp.float32))
    last = up_t is not None
    operands = [place, queries, *parts, *(state or ())]
    if last:
        operands.append(up_t)
        out = jax.ShapeDtypeStruct((HEADS_DEV * V_DIM, BLOCK), jnp.bfloat16)
    vmem = pl.BlockSpec(memory_space=pltpu.VMEM)
    rows = HEADS_DEV * BLOCK
    return pl.pallas_call(
        functools.partial(attend_kernel, len(parts), state is None, last),
        out_shape=out,
        in_specs=[pl.BlockSpec(memory_space=pltpu.SMEM)] + [vmem] * (len(operands) - 1),
        out_specs=vmem if last else (vmem,) * 3,
        scratch_shapes=[
            pltpu.VMEM((n_keys, 2 * BLOCK), jnp.float32),
            pltpu.VMEM((KV_RANK, n_keys), jnp.bfloat16),
        ],
        compiler_params=pltpu.CompilerParams(vmem_limit_bytes=VMEM_LIMIT),
        cost_estimate=pl.CostEstimate(
            flops=2 * rows * n_keys * (LAT + KV_RANK) * 2,
            bytes_accessed=4 * rows * KV_RANK * 2,
            transcendentals=rows * n_keys,
        ),
        name="attend",
    )(*operands)


def index_kernel(place_ref, query_ref, w_ref, own_ref, other_ref, out_ref, wb_ref, q_ref):
    core = place_ref[0]
    first_row = place_ref[1]
    rows = 16
    for head in range(IDX_HEADS):
        q_ref[head * rows : (head + 1) * rows, :] = query_ref[
            :, head * IDX_DIM : (head + 1) * IDX_DIM
        ]
        wb_ref[head * rows : (head + 1) * rows, :] = jnp.broadcast_to(
            w_ref[:, head : head + 1] * (IDX_DIM ** (-0.5)), (rows, BLOCK)
        )
    row_pos = first_row + lax.broadcasted_iota(jnp.int32, (rows, BLOCK), 0)
    lane = lax.broadcasted_iota(jnp.int32, (rows, BLOCK), 1)

    def chunk(keys_ref, parity, step):
        keys = keys_ref[pl.ds(step * 2, 2)].reshape(2 * BLOCK, IDX_DIM)
        dots = lax.dot_general(
            q_ref[...], keys, (((1,), (1,)), ((), ())), preferred_element_type=jnp.float32
        )
        for half in range(2):
            part = dots[:, half * BLOCK : (half + 1) * BLOCK]
            active = jnp.maximum(part, 0.0) * wb_ref[...]
            summed = jnp.sum(active.reshape(IDX_HEADS, rows, BLOCK), axis=0)
            start = pl.multiple_of(((step * 2 + half) * 2 + parity) * BLOCK, BLOCK)
            out_ref[:, pl.ds(start, BLOCK)] = jnp.where(start + lane <= row_pos, summed, 0.0)

    def one(step, carry):
        chunk(own_ref, core, step)
        chunk(other_ref, 1 - core, step)
        return carry

    lax.fori_loop(0, NBLK // 4, one, 0)


def index_part(place, query, weight, own, other):
    return pl.pallas_call(
        index_kernel,
        out_shape=jax.ShapeDtypeStruct((16, NBLK * BLOCK), jnp.float32),
        in_specs=[pl.BlockSpec(memory_space=pltpu.SMEM)]
        + [pl.BlockSpec(memory_space=pltpu.VMEM)] * 4,
        out_specs=pl.BlockSpec(memory_space=pltpu.VMEM),
        scratch_shapes=[
            pltpu.VMEM((IDX_HEADS * 16, BLOCK), jnp.float32),
            pltpu.VMEM((IDX_HEADS * 16, IDX_DIM), jnp.bfloat16),
        ],
        compiler_params=pltpu.CompilerParams(vmem_limit_bytes=VMEM_LIMIT),
        cost_estimate=pl.CostEstimate(
            flops=40_000_000_000, bytes_accessed=100 << 20, transcendentals=0
        ),
        name="index_scores",
    )(place, query, weight, own, other)


def prepare_kernel(lq_ref, up_ref, q_ref, up_t_ref):
    for head in range(HEADS_DEV):
        pair, half = divmod(head, 2)
        q_ref[pair, half * BLOCK : (half + 1) * BLOCK, :] = lq_ref[:, head * LAT : (head + 1) * LAT]
        up_t_ref[head] = up_ref[head].T


def prepare(latent_query, value_up):
    vmem = pl.BlockSpec(memory_space=pltpu.VMEM)
    shapes = [(HEADS_DEV // 2, 2 * BLOCK, LAT), (HEADS_DEV, V_DIM, KV_RANK)]
    return pl.pallas_call(
        prepare_kernel,
        out_shape=[jax.ShapeDtypeStruct(shape, jnp.bfloat16) for shape in shapes],
        in_specs=[vmem] * 2,
        out_specs=[vmem] * 2,
        compiler_params=pltpu.CompilerParams(vmem_limit_bytes=VMEM_LIMIT),
        cost_estimate=pl.CostEstimate(
            flops=80_000_000_000, bytes_accessed=200 << 20, transcendentals=0
        ),
        name="prepare",
    )(latent_query, value_up)


def arrange_kernel(z_ref, *refs):
    near, (w_ref, keys_ref) = refs[:NZ], refs[NZ:]
    for step in range(NZ):
        at = z_ref[0] ^ step
        w_ref[at] = near[step][16:, :]
        for block in range(8):
            keys_ref[at, block * 16 : (block + 1) * 16, :] = near[step][
                :16, block * BLOCK : (block + 1) * BLOCK
            ]


def arrange(z, near):
    vmem = pl.BlockSpec(memory_space=pltpu.VMEM)
    shapes = [(NZ, COLS, 1024), (NZ, BLOCK, IDX_DIM)]
    return pl.pallas_call(
        arrange_kernel,
        out_shape=[jax.ShapeDtypeStruct(shape, jnp.bfloat16) for shape in shapes],
        in_specs=[pl.BlockSpec(memory_space=pltpu.SMEM)] + [vmem] * NZ,
        out_specs=[vmem] * 2,
        compiler_params=pltpu.CompilerParams(vmem_limit_bytes=VMEM_LIMIT),
        name="arrange",
    )(z, *near)


def swap_core(value):
    return lax.ppermute(value, "c", [(0, 1), (1, 0)])


def spread(value, axis, count):
    wide = jnp.broadcast_to(value[None], (count,) + value.shape)
    return lax.all_to_all(wide, axis, 0, 0)


def body(
    index_query, index_weight, index_key, latent_query, latent, block_lists, value_up, out_weight
):
    y, z, core, x, w = (lax.axis_index(name) for name in ("y", "z", "c", "x", "w"))
    ctx_pos = (y * NZ + z) * NC + core
    head_pos = x * NW + w

    own = lax.dynamic_slice_in_dim(latent, x * 32, 32, 0).reshape(1, NC, 16, LAT)
    wide = jnp.broadcast_to(own, (NY * NZ, NC, 16, LAT)).reshape(NBLK, 16, LAT)

    key_rows = jnp.moveaxis(index_key.reshape(8, 16, IDX_DIM), 0, 1).reshape(16, 1024)
    packed = jnp.concatenate([key_rows, out_weight.T], axis=0)
    packed, wide = lax.optimization_barrier((packed, wide))
    near = [packed] + [
        lax.ppermute(packed, "z", [(at, at ^ step) for at in range(NZ)]) for step in range(1, NZ)
    ]
    pool = lax.all_to_all(wide, CTX, 0, 0)
    listed = block_lists[0]
    safe = jnp.maximum(listed, 0)
    both = jnp.concatenate([safe, swap_core(safe)])
    queries, up_t = prepare(latent_query, value_up)
    w_z, keys_z = arrange(z.reshape(1), near)
    w_all = lax.all_gather(w_z, "y", axis=0, tiled=True).reshape(NY * NZ * COLS, 1024)
    pool, queries, up_t, both = lax.optimization_barrier((pool, queries, up_t, both))

    picked = jnp.take(pool, both, axis=0, mode="clip").reshape(2, TOPK * 16, LAT)
    mine = jnp.concatenate([picked[0], swap_core(picked[1])], axis=0)
    up = [(at, (at + 1) % NX) for at in range(NX)]
    down = [(at, (at - 1) % NX) for at in range(NX)]
    left = lax.ppermute(mine, "x", up)
    right = lax.ppermute(mine, "x", down)

    def place(*xs):
        offsets = [((x + step) % NX) * 32 + 16 * (core ^ half) for step, half in xs]
        return jnp.concatenate([listed, jnp.stack([ctx_pos * BLOCK] + offsets)])

    places = (
        place((0, 0), (0, 1)),
        place((3, 0), (3, 1), (1, 0), (1, 1)),
        place((2, 0), (2, 1)),
    )
    state = attend(places[0], queries, [mine], None, None)
    left, right, state, keys_z = lax.optimization_barrier((left, right, state, keys_z))
    far_a = lax.ppermute(left[:256], "x", up)
    far_b = lax.ppermute(right[256:], "x", down)
    keys_own = spread(keys_z, "y", NY).reshape(NY * NZ, BLOCK, IDX_DIM)
    state = attend(places[1], queries, [left, right], state, None)
    far_a, far_b, state, keys_own = lax.optimization_barrier((far_a, far_b, state, keys_own))
    keys_other = swap_core(keys_own)
    values = attend(places[2], queries, [far_a, far_b], state, up_t)

    values, keys_other = lax.optimization_barrier((values, keys_other))

    both_values = jnp.concatenate([values, swap_core(values)], axis=1)
    terms = jnp.dot(w_all, both_values, preferred_element_type=jnp.float32).astype(jnp.bfloat16)
    terms = terms.reshape(NY, NZ * COLS, 2 * BLOCK)
    shares = lax.all_to_all(terms, HEAD, 0, 0)
    first_row = ctx_pos * TOK_DEV + head_pos * 16
    index_scores = index_part(
        jnp.stack([core, first_row]), index_query, index_weight, keys_own, keys_other
    )
    shares, index_scores = lax.optimization_barrier((shares, index_scores))
    summed = jnp.sum(shares.astype(jnp.float32), axis=0).astype(jnp.bfloat16)
    kept = summed[:, :BLOCK].reshape(NZ, COLS, BLOCK)
    other = swap_core(summed[:, BLOCK:]).reshape(NZ, COLS, BLOCK)
    first = jnp.where(core == 0, kept, other)
    second = jnp.where(core == 0, other, kept)
    attn_out = jnp.stack([first, second], axis=1).reshape(NZ * NC * COLS, BLOCK).T

    return index_scores, attn_out


def solution(mesh):
    fine = Mesh(mesh.devices.reshape(NY, NZ, NC, NX, NW), ("y", "z", "c", "x", "w"))
    return jax.shard_map(
        body,
        mesh=fine,
        in_specs=(
            P(CTX + HEAD, None),
            P(CTX + HEAD, None),
            P(CTX, None),
            P(CTX, HEAD),
            P(CTX, None),
            P(CTX, None),
            P(HEAD, None, None),
            P(HEAD, CTX),
        ),
        out_specs=(P(CTX + HEAD, None), P(CTX, HEAD)),
        check_vma=False,
    )
```

```python
import functools

import jax
import jax.numpy as jnp
from jax import lax
from jax.experimental import pallas as pl
from jax.experimental.pallas import tpu as pltpu
from jax.sharding import Mesh
from jax.sharding import PartitionSpec as P

TOK_DEV = 128
HEADS_DEV = 8
KV_RANK = 512
LAT = 576
V_DIM = 128
IDX_HEADS = 32
IDX_DIM = 128
BLOCK = 128
TOPK = 16
NBLK = 64
COLS = 56
NY, NZ, NC, NX, NW = 8, 4, 2, 4, 2

CTX = ("y", "z", "c")
HEAD = ("x", "w")
LOG2E = 1.4426950408889634
SCORE_SCALE = 192.0 ** (-0.5) * LOG2E
MASKED = -1e30
VMEM_LIMIT = 56 * 1024 * 1024


def attend_kernel(count, first, last, *refs):
    place_ref, q_ref = refs[:2]
    kv_refs = refs[2 : 2 + count]
    refs = refs[2 + count :]
    if not first:
        max_in, total_in, sum_in = refs[:3]
        refs = refs[3:]
    if last:
        up_ref, out_ref = refs[:2]
        refs = refs[2:]
    else:
        max_out, total_out, sum_out = refs[:3]
        refs = refs[3:]
    bias_ref, vt_ref = refs
    keys = jnp.concatenate([ref[...] for ref in kv_refs], axis=0)
    n_keys = keys.shape[0]
    vt_ref[...] = keys[:, :KV_RANK].T
    row = lax.broadcasted_iota(jnp.int32, (16, BLOCK), 0)
    query = place_ref[TOPK] + lax.broadcasted_iota(jnp.int32, (16, BLOCK), 1)
    for group in range(n_keys // 16):
        part, slot = divmod(group, TOPK)
        entry = place_ref[slot]
        start = jnp.where(entry < 0, 2 * NBLK, entry) * BLOCK + place_ref[TOPK + 1 + part]
        seen = jnp.where(start + row <= query, 0.0, MASKED)
        bias_ref[group * 16 : (group + 1) * 16, :BLOCK] = seen
        bias_ref[group * 16 : (group + 1) * 16, BLOCK:] = seen
    for pair in range(HEADS_DEV // 2):
        scores = lax.dot_general(
            keys, q_ref[pair], (((1,), (1,)), ((), ())), preferred_element_type=jnp.float32
        )
        scores = scores + bias_ref[...]
        row_max = jnp.max(scores, axis=0, keepdims=True)
        if not first:
            row_max = jnp.maximum(row_max, max_in[pair])
            keep = jnp.exp2((max_in[pair] - row_max) * SCORE_SCALE)
        expo = jnp.exp2((scores - row_max) * SCORE_SCALE)
        total = jnp.sum(expo, axis=0, keepdims=True)
        lat_sum = lax.dot_general(
            vt_ref[...],
            expo.astype(jnp.bfloat16),
            (((1,), (0,)), ((), ())),
            preferred_element_type=jnp.float32,
        )
        if not first:
            total = total + total_in[pair] * keep
            lat_sum = lat_sum + sum_in[pair] * keep
        if not last:
            max_out[pair] = row_max
            total_out[pair] = total
            sum_out[pair] = lat_sum
            continue
        lat_out = (lat_sum / total).astype(jnp.bfloat16)
        for half in range(2):
            head = 2 * pair + half
            values = lax.dot_general(
                up_ref[head],
                lat_out[:, half * BLOCK : (half + 1) * BLOCK],
                (((1,), (0,)), ((), ())),
                preferred_element_type=jnp.float32,
            )
            out_ref[head * V_DIM : (head + 1) * V_DIM, :] = values.astype(jnp.bfloat16)


def attend(place, queries, parts, state, up_t):
    pairs = HEADS_DEV // 2
    n_keys = sum(part.shape[0] for part in parts)
    stat = jax.ShapeDtypeStruct((pairs, 1, 2 * BLOCK), jnp.float32)
    out = (stat, stat, jax.ShapeDtypeStruct((pairs, KV_RANK, 2 * BLOCK), jnp.float32))
    last = up_t is not None
    operands = [place, queries, *parts, *(state or ())]
    if last:
        operands.append(up_t)
        out = jax.ShapeDtypeStruct((HEADS_DEV * V_DIM, BLOCK), jnp.bfloat16)
    vmem = pl.BlockSpec(memory_space=pltpu.VMEM)
    rows = HEADS_DEV * BLOCK
    return pl.pallas_call(
        functools.partial(attend_kernel, len(parts), state is None, last),
        out_shape=out,
        in_specs=[pl.BlockSpec(memory_space=pltpu.SMEM)] + [vmem] * (len(operands) - 1),
        out_specs=vmem if last else (vmem,) * 3,
        scratch_shapes=[
            pltpu.VMEM((n_keys, 2 * BLOCK), jnp.float32),
            pltpu.VMEM((KV_RANK, n_keys), jnp.bfloat16),
        ],
        compiler_params=pltpu.CompilerParams(vmem_limit_bytes=VMEM_LIMIT),
        cost_estimate=pl.CostEstimate(
            flops=40_000_000_000,
            bytes_accessed=4 * rows * KV_RANK * 2,
            transcendentals=rows * n_keys,
        ),
        name="attend",
    )(*operands)


def index_kernel(place_ref, query_ref, w_ref, own_ref, other_ref, out_ref, wb_ref, q_ref):
    core = place_ref[0]
    first_row = place_ref[1]
    rows = 16
    for head in range(IDX_HEADS):
        q_ref[head * rows : (head + 1) * rows, :] = query_ref[
            :, head * IDX_DIM : (head + 1) * IDX_DIM
        ]
        wb_ref[head * rows : (head + 1) * rows, :] = jnp.broadcast_to(
            w_ref[:, head : head + 1] * (IDX_DIM ** (-0.5)), (rows, BLOCK)
        )
    row_pos = first_row + lax.broadcasted_iota(jnp.int32, (rows, BLOCK), 0)
    lane = lax.broadcasted_iota(jnp.int32, (rows, BLOCK), 1)

    def chunk(keys_ref, parity, step):
        keys = keys_ref[pl.ds(step * 2, 2)].reshape(2 * BLOCK, IDX_DIM)
        dots = lax.dot_general(
            q_ref[...], keys, (((1,), (1,)), ((), ())), preferred_element_type=jnp.float32
        )
        for half in range(2):
            part = dots[:, half * BLOCK : (half + 1) * BLOCK]
            active = jnp.maximum(part, 0.0) * wb_ref[...]
            summed = jnp.sum(active.reshape(IDX_HEADS, rows, BLOCK), axis=0)
            start = pl.multiple_of(((step * 2 + half) * 2 + parity) * BLOCK, BLOCK)
            out_ref[:, pl.ds(start, BLOCK)] = jnp.where(start + lane <= row_pos, summed, 0.0)

    def one(step, carry):
        chunk(own_ref, core, step)
        chunk(other_ref, 1 - core, step)
        return carry

    lax.fori_loop(0, NBLK // 4, one, 0)


def index_part(place, query, weight, own, other):
    return pl.pallas_call(
        index_kernel,
        out_shape=jax.ShapeDtypeStruct((16, NBLK * BLOCK), jnp.float32),
        in_specs=[pl.BlockSpec(memory_space=pltpu.SMEM)]
        + [pl.BlockSpec(memory_space=pltpu.VMEM)] * 4,
        out_specs=pl.BlockSpec(memory_space=pltpu.VMEM),
        scratch_shapes=[
            pltpu.VMEM((IDX_HEADS * 16, BLOCK), jnp.float32),
            pltpu.VMEM((IDX_HEADS * 16, IDX_DIM), jnp.bfloat16),
        ],
        compiler_params=pltpu.CompilerParams(vmem_limit_bytes=VMEM_LIMIT),
        cost_estimate=pl.CostEstimate(
            flops=40_000_000_000, bytes_accessed=100 << 20, transcendentals=0
        ),
        name="index_scores",
    )(place, query, weight, own, other)


def prepare_kernel(lq_ref, up_ref, q_ref, up_t_ref):
    for head in range(HEADS_DEV):
        pair, half = divmod(head, 2)
        q_ref[pair, half * BLOCK : (half + 1) * BLOCK, :] = lq_ref[:, head * LAT : (head + 1) * LAT]
        up_t_ref[head] = up_ref[head].T


def prepare(latent_query, value_up):
    vmem = pl.BlockSpec(memory_space=pltpu.VMEM)
    shapes = [(HEADS_DEV // 2, 2 * BLOCK, LAT), (HEADS_DEV, V_DIM, KV_RANK)]
    return pl.pallas_call(
        prepare_kernel,
        out_shape=[jax.ShapeDtypeStruct(shape, jnp.bfloat16) for shape in shapes],
        in_specs=[vmem] * 2,
        out_specs=[vmem] * 2,
        compiler_params=pltpu.CompilerParams(vmem_limit_bytes=VMEM_LIMIT),
        cost_estimate=pl.CostEstimate(
            flops=20_000_000_000, bytes_accessed=20_000_000, transcendentals=0
        ),
        name="prepare",
    )(latent_query, value_up)


def arrange_kernel(z_ref, *refs):
    near, (w_ref, keys_ref) = refs[:NZ], refs[NZ:]
    for step in range(NZ):
        at = z_ref[0] ^ step
        w_ref[at] = near[step][16:, :]
        for block in range(8):
            keys_ref[at, block * 16 : (block + 1) * 16, :] = near[step][
                :16, block * BLOCK : (block + 1) * BLOCK
            ]


def arrange(z, near):
    vmem = pl.BlockSpec(memory_space=pltpu.VMEM)
    shapes = [(NZ, COLS, 1024), (NZ, BLOCK, IDX_DIM)]
    return pl.pallas_call(
        arrange_kernel,
        out_shape=[jax.ShapeDtypeStruct(shape, jnp.bfloat16) for shape in shapes],
        in_specs=[pl.BlockSpec(memory_space=pltpu.SMEM)] + [vmem] * NZ,
        out_specs=[vmem] * 2,
        compiler_params=pltpu.CompilerParams(vmem_limit_bytes=VMEM_LIMIT),
        name="arrange",
    )(z, *near)


def swap_core(value):
    return lax.ppermute(value, "c", [(0, 1), (1, 0)])


def spread(value, axis, count):
    wide = jnp.broadcast_to(value[None], (count,) + value.shape)
    return lax.all_to_all(wide, axis, 0, 0)


def body(
    index_query, index_weight, index_key, latent_query, latent, block_lists, value_up, out_weight
):
    y, z, core, x, w = (lax.axis_index(name) for name in ("y", "z", "c", "x", "w"))
    ctx_pos = (y * NZ + z) * NC + core
    head_pos = x * NW + w

    own = lax.dynamic_slice_in_dim(latent, x * 32, 32, 0).reshape(1, NC, 16, LAT)
    wide = jnp.broadcast_to(own, (NY * NZ, NC, 16, LAT)).reshape(NBLK, 16, LAT)

    key_rows = jnp.moveaxis(index_key.reshape(8, 16, IDX_DIM), 0, 1).reshape(16, 1024)
    packed = jnp.concatenate([key_rows, out_weight.T], axis=0)
    near = [packed] + [
        lax.ppermute(packed, "z", [(at, at ^ step) for at in range(NZ)]) for step in range(1, NZ)
    ]
    pool = lax.all_to_all(wide, CTX, 0, 0)
    listed = block_lists[0]
    safe = jnp.maximum(listed, 0)
    both = jnp.concatenate([safe, swap_core(safe)])
    queries, up_t = prepare(latent_query, value_up)
    w_z, keys_z = arrange(z.reshape(1), near)
    w_all = lax.all_gather(w_z, "y", axis=0, tiled=True).reshape(NY * NZ * COLS, 1024)
    pool, queries, up_t, both, keys_z = lax.optimization_barrier(
        (pool, queries, up_t, both, keys_z)
    )

    picked = jnp.take(pool, both, axis=0, mode="clip").reshape(2, TOPK * 16, LAT)
    mine = jnp.concatenate([picked[0], swap_core(picked[1])], axis=0)
    up = [(at, (at + 1) % NX) for at in range(NX)]
    down = [(at, (at - 1) % NX) for at in range(NX)]
    left = lax.ppermute(mine, "x", up)
    right = lax.ppermute(mine, "x", down)

    def place(*xs):
        offsets = [((x + step) % NX) * 32 + 16 * (core ^ half) for step, half in xs]
        return jnp.concatenate([listed, jnp.stack([ctx_pos * BLOCK] + offsets)])

    places = (
        place((0, 0), (0, 1)),
        place((3, 0), (3, 1), (1, 0), (1, 1)),
        place((2, 0), (2, 1)),
    )
    state = attend(places[0], queries, [mine], None, None)
    left, right, state, keys_z = lax.optimization_barrier((left, right, state, keys_z))
    far_a = lax.ppermute(left[:256], "x", up)
    far_b = lax.ppermute(right[256:], "x", down)
    keys_own = lax.all_gather(keys_z, "y", axis=0, tiled=True)
    state = attend(places[1], queries, [left, right], state, None)
    far_a, far_b, state = lax.optimization_barrier((far_a, far_b, state))
    values = attend(places[2], queries, [far_a, far_b], state, up_t)

    both_values = jnp.concatenate([values, swap_core(values)], axis=1)
    terms = jnp.dot(w_all, both_values, preferred_element_type=jnp.float32).astype(jnp.bfloat16)
    terms = terms.reshape(NY, NZ * COLS, 2 * BLOCK)
    first_row = ctx_pos * TOK_DEV + head_pos * 16
    terms, keys_own = lax.optimization_barrier((terms, keys_own))
    keys_other = swap_core(keys_own)
    index_scores = index_part(
        jnp.stack([core, first_row]), index_query, index_weight, keys_own, keys_other
    )
    shares = lax.all_to_all(terms, HEAD, 0, 0)
    shares, index_scores = lax.optimization_barrier((shares, index_scores))
    summed = jnp.sum(shares.astype(jnp.float32), axis=0).astype(jnp.bfloat16)
    kept = summed[:, :BLOCK].reshape(NZ, COLS, BLOCK)
    other = swap_core(summed[:, BLOCK:]).reshape(NZ, COLS, BLOCK)
    first = jnp.where(core == 0, kept, other)
    second = jnp.where(core == 0, other, kept)
    attn_out = jnp.stack([first, second], axis=1).reshape(NZ * NC * COLS, BLOCK).T

    return index_scores, attn_out


def solution(mesh):
    fine = Mesh(mesh.devices.reshape(NY, NZ, NC, NX, NW), ("y", "z", "c", "x", "w"))
    return jax.shard_map(
        body,
        mesh=fine,
        in_specs=(
            P(CTX + HEAD, None),
            P(CTX + HEAD, None),
            P(CTX, None),
            P(CTX, HEAD),
            P(CTX, None),
            P(CTX, None),
            P(HEAD, None, None),
            P(HEAD, CTX),
        ),
        out_specs=(P(CTX + HEAD, None), P(CTX, HEAD)),
        check_vma=False,
    )
```

```python
import functools

import jax
import jax.numpy as jnp
from jax import lax
from jax.experimental import pallas as pl
from jax.experimental.pallas import tpu as pltpu
from jax.sharding import Mesh
from jax.sharding import PartitionSpec as P

TOK_DEV = 128
HEADS_DEV = 8
KV_RANK = 512
LAT = 576
V_DIM = 128
IDX_HEADS = 32
IDX_DIM = 128
BLOCK = 128
TOPK = 16
NBLK = 64
ROWS = 8
PACKED = 72
COLS = 56
NY, NZ, NC, NX, NW = 8, 4, 2, 4, 2

CTX = ("y", "z", "c")
HEAD = ("x", "w")
LOG2E = 1.4426950408889634
SCORE_SCALE = 192.0 ** (-0.5) * LOG2E
MASKED = -1e30
VMEM_LIMIT = 56 * 1024 * 1024


def attend_kernel(count, first, last, *refs):
    place_ref, q_ref = refs[:2]
    kv_refs = refs[2 : 2 + count]
    refs = refs[2 + count :]
    if not first:
        max_in, total_in, sum_in = refs[:3]
        refs = refs[3:]
    if last:
        up_ref, out_ref = refs[:2]
        refs = refs[2:]
    else:
        max_out, total_out, sum_out = refs[:3]
        refs = refs[3:]
    bias_ref, vt_ref = refs
    keys = jnp.concatenate([ref[...] for ref in kv_refs], axis=0)
    n_keys = keys.shape[0]
    vt_ref[...] = keys[:, :KV_RANK].T
    row = lax.broadcasted_iota(jnp.int32, (ROWS, BLOCK), 0)
    query = place_ref[TOPK] + lax.broadcasted_iota(jnp.int32, (ROWS, BLOCK), 1)
    for group in range(n_keys // ROWS):
        part, slot = divmod(group, TOPK)
        entry = place_ref[slot]
        start = jnp.where(entry < 0, 2 * NBLK, entry) * BLOCK + place_ref[TOPK + 1 + part]
        seen = jnp.where(start + row <= query, 0.0, MASKED)
        bias_ref[group * ROWS : (group + 1) * ROWS, :BLOCK] = seen
        bias_ref[group * ROWS : (group + 1) * ROWS, BLOCK:] = seen
    for pair in range(HEADS_DEV // 2):
        scores = lax.dot_general(
            keys, q_ref[pair], (((1,), (1,)), ((), ())), preferred_element_type=jnp.float32
        )
        scores = scores + bias_ref[...]
        row_max = jnp.max(scores, axis=0, keepdims=True)
        if not first:
            row_max = jnp.maximum(row_max, max_in[pair])
            keep = jnp.exp2((max_in[pair] - row_max) * SCORE_SCALE)
        expo = jnp.exp2((scores - row_max) * SCORE_SCALE)
        total = jnp.sum(expo, axis=0, keepdims=True)
        lat_sum = lax.dot_general(
            vt_ref[...],
            expo.astype(jnp.bfloat16),
            (((1,), (0,)), ((), ())),
            preferred_element_type=jnp.float32,
        )
        if not first:
            total = total + total_in[pair] * keep
            lat_sum = lat_sum + sum_in[pair] * keep
        if not last:
            max_out[pair] = row_max
            total_out[pair] = total
            sum_out[pair] = lat_sum
            continue
        lat_out = (lat_sum / total).astype(jnp.bfloat16)
        for half in range(2):
            head = 2 * pair + half
            values = lax.dot_general(
                up_ref[head],
                lat_out[:, half * BLOCK : (half + 1) * BLOCK],
                (((1,), (0,)), ((), ())),
                preferred_element_type=jnp.float32,
            )
            out_ref[head * V_DIM : (head + 1) * V_DIM, :] = values.astype(jnp.bfloat16)


def attend(place, queries, parts, state, up_t):
    pairs = HEADS_DEV // 2
    n_keys = sum(part.shape[0] for part in parts)
    stat = jax.ShapeDtypeStruct((pairs, 1, 2 * BLOCK), jnp.float32)
    out = (stat, stat, jax.ShapeDtypeStruct((pairs, KV_RANK, 2 * BLOCK), jnp.float32))
    last = up_t is not None
    operands = [place, queries, *parts, *(state or ())]
    if last:
        operands.append(up_t)
        out = jax.ShapeDtypeStruct((HEADS_DEV * V_DIM, BLOCK), jnp.bfloat16)
    vmem = pl.BlockSpec(memory_space=pltpu.VMEM)
    rows = HEADS_DEV * BLOCK
    return pl.pallas_call(
        functools.partial(attend_kernel, len(parts), state is None, last),
        out_shape=out,
        in_specs=[pl.BlockSpec(memory_space=pltpu.SMEM)] + [vmem] * (len(operands) - 1),
        out_specs=vmem if last else (vmem,) * 3,
        scratch_shapes=[
            pltpu.VMEM((n_keys, 2 * BLOCK), jnp.float32),
            pltpu.VMEM((KV_RANK, n_keys), jnp.bfloat16),
        ],
        compiler_params=pltpu.CompilerParams(vmem_limit_bytes=VMEM_LIMIT),
        cost_estimate=pl.CostEstimate(
            flops=20000000000,
            bytes_accessed=4 * rows * KV_RANK * 2,
            transcendentals=rows * n_keys,
        ),
        name="attend",
    )(*operands)


def index_kernel(place_ref, query_ref, w_ref, own_ref, other_ref, out_ref, wb_ref, q_ref):
    core = place_ref[0]
    first_row = place_ref[1]
    rows = 16
    for head in range(IDX_HEADS):
        q_ref[head * rows : (head + 1) * rows, :] = query_ref[
            :, head * IDX_DIM : (head + 1) * IDX_DIM
        ]
        wb_ref[head * rows : (head + 1) * rows, :] = jnp.broadcast_to(
            w_ref[:, head : head + 1] * (IDX_DIM ** (-0.5)), (rows, BLOCK)
        )
    row_pos = first_row + lax.broadcasted_iota(jnp.int32, (rows, BLOCK), 0)
    lane = lax.broadcasted_iota(jnp.int32, (rows, BLOCK), 1)

    def chunk(keys_ref, parity, step):
        keys = jnp.concatenate(
            [
                keys_ref[step * 2 + half, :, at * IDX_DIM : (at + 1) * IDX_DIM]
                for half in range(2)
                for at in range(8)
            ],
            axis=0,
        )
        dots = lax.dot_general(
            q_ref[...], keys, (((1,), (1,)), ((), ())), preferred_element_type=jnp.float32
        )
        for half in range(2):
            part = dots[:, half * BLOCK : (half + 1) * BLOCK]
            active = jnp.maximum(part, 0.0) * wb_ref[...]
            summed = jnp.sum(active.reshape(IDX_HEADS, rows, BLOCK), axis=0)
            start = pl.multiple_of(((step * 2 + half) * 2 + parity) * BLOCK, BLOCK)
            out_ref[:, pl.ds(start, BLOCK)] = jnp.where(start + lane <= row_pos, summed, 0.0)

    def one(step, carry):
        chunk(own_ref, core, step)
        chunk(other_ref, 1 - core, step)
        return carry

    lax.fori_loop(0, NBLK // 4, one, 0)


def index_part(place, query, weight, own, other):
    return pl.pallas_call(
        index_kernel,
        out_shape=jax.ShapeDtypeStruct((16, NBLK * BLOCK), jnp.float32),
        in_specs=[pl.BlockSpec(memory_space=pltpu.SMEM)]
        + [pl.BlockSpec(memory_space=pltpu.VMEM)] * 4,
        out_specs=pl.BlockSpec(memory_space=pltpu.VMEM),
        scratch_shapes=[
            pltpu.VMEM((IDX_HEADS * 16, BLOCK), jnp.float32),
            pltpu.VMEM((IDX_HEADS * 16, IDX_DIM), jnp.bfloat16),
        ],
        compiler_params=pltpu.CompilerParams(vmem_limit_bytes=VMEM_LIMIT),
        cost_estimate=pl.CostEstimate(
            flops=40_000_000_000, bytes_accessed=100 << 20, transcendentals=0
        ),
        name="index_scores",
    )(place, query, weight, own, other)


def prepare_kernel(lq_ref, up_ref, q_ref, up_t_ref):
    for head in range(HEADS_DEV):
        pair, half = divmod(head, 2)
        q_ref[pair, half * BLOCK : (half + 1) * BLOCK, :] = lq_ref[:, head * LAT : (head + 1) * LAT]
        up_t_ref[head] = up_ref[head].T


def prepare(latent_query, value_up):
    vmem = pl.BlockSpec(memory_space=pltpu.VMEM)
    shapes = [(HEADS_DEV // 2, 2 * BLOCK, LAT), (HEADS_DEV, V_DIM, KV_RANK)]
    return pl.pallas_call(
        prepare_kernel,
        out_shape=[jax.ShapeDtypeStruct(shape, jnp.bfloat16) for shape in shapes],
        in_specs=[vmem] * 2,
        out_specs=[vmem] * 2,
        compiler_params=pltpu.CompilerParams(vmem_limit_bytes=VMEM_LIMIT),
        cost_estimate=pl.CostEstimate(
            flops=1000000000, bytes_accessed=4000000, transcendentals=0
        ),
        name="prepare",
    )(latent_query, value_up)


def arrange_kernel(z_ref, *refs):
    out_ref = refs[NZ]
    for step in range(NZ):
        out_ref[z_ref[0] ^ step] = refs[step][...]


def arrange(z, near):
    vmem = pl.BlockSpec(memory_space=pltpu.VMEM)
    return pl.pallas_call(
        arrange_kernel,
        out_shape=jax.ShapeDtypeStruct((NZ, PACKED, 1024), jnp.bfloat16),
        in_specs=[pl.BlockSpec(memory_space=pltpu.SMEM)] + [vmem] * NZ,
        out_specs=vmem,
        compiler_params=pltpu.CompilerParams(vmem_limit_bytes=VMEM_LIMIT),
        name="arrange",
    )(z, *near)


def project_kernel(w_ref, own_ref, other_ref, out_ref):
    weights = w_ref[...].reshape(NZ * PACKED, 1024)
    for half, values_ref in enumerate((own_ref, other_ref)):
        terms = lax.dot_general(
            weights, values_ref[...], (((1,), (0,)), ((), ())), preferred_element_type=jnp.float32
        )
        terms = terms.reshape(NZ, PACKED, BLOCK)[:, 16:, :].reshape(NZ * COLS, BLOCK)
        out_ref[0, :, half * BLOCK : (half + 1) * BLOCK] = terms.astype(jnp.bfloat16)


def project(gathered, own, other):
    values = pl.BlockSpec((HEADS_DEV * V_DIM, BLOCK), lambda i: (0, 0))
    return pl.pallas_call(
        project_kernel,
        out_shape=jax.ShapeDtypeStruct((NY, NZ * COLS, 2 * BLOCK), jnp.bfloat16),
        grid=(NY,),
        in_specs=[pl.BlockSpec((NZ, PACKED, 1024), lambda i: (i, 0, 0)), values, values],
        out_specs=pl.BlockSpec((1, NZ * COLS, 2 * BLOCK), lambda i: (i, 0, 0)),
        compiler_params=pltpu.CompilerParams(vmem_limit_bytes=VMEM_LIMIT),
        name="project",
    )(gathered, own, other)


def swap_core(value):
    return lax.ppermute(value, "c", [(0, 1), (1, 0)])


def spread(value, axis, count):
    wide = jnp.broadcast_to(value[None], (count,) + value.shape)
    return lax.all_to_all(wide, axis, 0, 0)


def body(
    index_query, index_weight, index_key, latent_query, latent, block_lists, value_up, out_weight
):
    y, z, core, x, w = (lax.axis_index(name) for name in ("y", "z", "c", "x", "w"))
    ctx_pos = (y * NZ + z) * NC + core
    head_pos = x * NW + w

    own = lax.dynamic_slice_in_dim(latent, head_pos * 16, 16, 0).reshape(1, NC, ROWS, LAT)
    wide = jnp.broadcast_to(own, (NY * NZ, NC, ROWS, LAT)).reshape(NBLK, ROWS, LAT)

    key_rows = jnp.moveaxis(index_key.reshape(8, 16, IDX_DIM), 0, 1).reshape(16, 1024)
    packed = jnp.concatenate([key_rows, out_weight.T], axis=0)
    near = [packed] + [
        lax.ppermute(packed, "z", [(at, at ^ step) for at in range(NZ)]) for step in range(1, NZ)
    ]
    pool = lax.all_to_all(wide, CTX, 0, 0)
    listed = block_lists[0]
    safe = jnp.maximum(listed, 0)
    both = jnp.concatenate([safe, swap_core(safe)])
    queries, up_t = prepare(latent_query, value_up)
    near_z = arrange(z.reshape(1), near)
    pool, queries, up_t, both, near_z = lax.optimization_barrier(
        (pool, queries, up_t, both, near_z)
    )
    gathered = lax.all_gather(near_z, "y", axis=0, tiled=True)

    picked = jnp.take(pool, both, axis=0, mode="clip").reshape(2, TOPK * ROWS, LAT)
    mine = jnp.concatenate([picked[0], swap_core(picked[1])], axis=0)
    mine = jnp.concatenate([mine, lax.ppermute(mine, "w", [(0, 1), (1, 0)])], axis=0)
    up = [(at, (at + 1) % NX) for at in range(NX)]
    down = [(at, (at - 1) % NX) for at in range(NX)]
    left = lax.ppermute(mine, "x", up)
    right = lax.ppermute(mine, "x", down)

    def place(*parts):
        offsets = [
            ((x + step) % NX) * 32 + (w ^ far) * 16 + (core ^ half) * ROWS
            for step, far in parts
            for half in range(NC)
        ]
        return jnp.concatenate([listed, jnp.stack([ctx_pos * BLOCK] + offsets)])

    places = (
        place((0, 0), (0, 1)),
        place((3, 0), (3, 1), (1, 0), (1, 1)),
        place((2, 0), (2, 1)),
    )
    state = attend(places[0], queries, [mine], None, None)
    left, right, state = lax.optimization_barrier((left, right, state))
    far_a = lax.ppermute(left[:256], "x", up)
    far_b = lax.ppermute(right[256:], "x", down)
    state = attend(places[1], queries, [left, right], state, None)
    far_a, far_b, state = lax.optimization_barrier((far_a, far_b, state))
    values = attend(places[2], queries, [far_a, far_b], state, up_t)

    values, gathered = lax.optimization_barrier((values, gathered))
    terms = project(gathered, values, swap_core(values))
    keys_own = gathered[:, :16]
    first_row = ctx_pos * TOK_DEV + head_pos * 16
    keys_other = swap_core(keys_own)
    index_scores = index_part(
        jnp.stack([core, first_row]), index_query, index_weight, keys_own, keys_other
    )
    shares = lax.all_to_all(terms, HEAD, 0, 0)
    shares, index_scores = lax.optimization_barrier((shares, index_scores))
    summed = jnp.sum(shares.astype(jnp.float32), axis=0).astype(jnp.bfloat16)
    kept = summed[:, :BLOCK].reshape(NZ, COLS, BLOCK)
    other = swap_core(summed[:, BLOCK:]).reshape(NZ, COLS, BLOCK)
    first = jnp.where(core == 0, kept, other)
    second = jnp.where(core == 0, other, kept)
    attn_out = jnp.stack([first, second], axis=1).reshape(NZ * NC * COLS, BLOCK).T

    return index_scores, attn_out


def solution(mesh):
    fine = Mesh(mesh.devices.reshape(NY, NZ, NC, NX, NW), ("y", "z", "c", "x", "w"))
    return jax.shard_map(
        body,
        mesh=fine,
        in_specs=(
            P(CTX + HEAD, None),
            P(CTX + HEAD, None),
            P(CTX, None),
            P(CTX, HEAD),
            P(CTX, None),
            P(CTX, None),
            P(HEAD, None, None),
            P(HEAD, CTX),
        ),
        out_specs=(P(CTX + HEAD, None), P(CTX, HEAD)),
        check_vma=False,
    )
```

```python
import functools

import jax
import jax.numpy as jnp
from jax import lax
from jax.experimental import pallas as pl
from jax.experimental.pallas import tpu as pltpu
from jax.sharding import Mesh
from jax.sharding import PartitionSpec as P

TOK_DEV = 128
HEADS_DEV = 8
KV_RANK = 512
LAT = 576
V_DIM = 128
IDX_HEADS = 32
IDX_DIM = 128
BLOCK = 128
TOPK = 16
NBLK = 64
ROWS = 8
PACKED = 72
COLS = 56
NY, NZ, NC, NX, NW = 8, 4, 2, 4, 2

CTX = ("y", "z", "c")
HEAD = ("x", "w")
LOG2E = 1.4426950408889634
SCORE_SCALE = 192.0 ** (-0.5) * LOG2E
MASKED = -1e30
VMEM_LIMIT = 56 * 1024 * 1024


def attend_kernel(start, count, first, last, *refs):
    place_ref, q_ref = refs[:2]
    kv_refs = refs[2 : 2 + count]
    refs = refs[2 + count :]
    if not first:
        max_in, total_in, sum_in = refs[:3]
        refs = refs[3:]
    if last:
        up_ref, out_ref = refs[:2]
        refs = refs[2:]
    else:
        max_out, total_out, sum_out = refs[:3]
        refs = refs[3:]
    bias_ref, vt_ref = refs
    keys = jnp.concatenate([ref[...] for ref in kv_refs], axis=0)
    n_keys = keys.shape[0]
    vt_ref[...] = keys[:, :KV_RANK].T
    row = lax.broadcasted_iota(jnp.int32, (ROWS, BLOCK), 0)
    query = place_ref[TOPK] + lax.broadcasted_iota(jnp.int32, (ROWS, BLOCK), 1)
    for group in range(n_keys // ROWS):
        part, slot = divmod(group, TOPK)
        entry = place_ref[slot]
        first_key = jnp.where(entry < 0, 2 * NBLK, entry) * BLOCK
        first_key = first_key + place_ref[TOPK + 1 + start + part]
        seen = jnp.where(first_key + row <= query, 0.0, MASKED)
        bias_ref[group * ROWS : (group + 1) * ROWS, :BLOCK] = seen
        bias_ref[group * ROWS : (group + 1) * ROWS, BLOCK:] = seen
    for pair in range(HEADS_DEV // 2):
        scores = lax.dot_general(
            keys, q_ref[pair], (((1,), (1,)), ((), ())), preferred_element_type=jnp.float32
        )
        scores = scores + bias_ref[...]
        row_max = jnp.max(scores, axis=0, keepdims=True)
        if not first:
            row_max = jnp.maximum(row_max, max_in[pair])
            keep = jnp.exp2((max_in[pair] - row_max) * SCORE_SCALE)
        expo = jnp.exp2((scores - row_max) * SCORE_SCALE)
        total = jnp.sum(expo, axis=0, keepdims=True)
        lat_sum = lax.dot_general(
            vt_ref[...],
            expo.astype(jnp.bfloat16),
            (((1,), (0,)), ((), ())),
            preferred_element_type=jnp.float32,
        )
        if not first:
            total = total + total_in[pair] * keep
            lat_sum = lat_sum + sum_in[pair] * keep
        if not last:
            max_out[pair] = row_max
            total_out[pair] = total
            sum_out[pair] = lat_sum
            continue
        lat_out = (lat_sum / total).astype(jnp.bfloat16)
        for half in range(2):
            head = 2 * pair + half
            values = lax.dot_general(
                up_ref[head],
                lat_out[:, half * BLOCK : (half + 1) * BLOCK],
                (((1,), (0,)), ((), ())),
                preferred_element_type=jnp.float32,
            )
            out_ref[head * V_DIM : (head + 1) * V_DIM, :] = values.astype(jnp.bfloat16)


def attend(start, place, queries, parts, state, up_t):
    pairs = HEADS_DEV // 2
    n_keys = sum(part.shape[0] for part in parts)
    stat = jax.ShapeDtypeStruct((pairs, 1, 2 * BLOCK), jnp.float32)
    out = (stat, stat, jax.ShapeDtypeStruct((pairs, KV_RANK, 2 * BLOCK), jnp.float32))
    last = up_t is not None
    operands = [place, queries, *parts, *(state or ())]
    if last:
        operands.append(up_t)
        out = jax.ShapeDtypeStruct((HEADS_DEV * V_DIM, BLOCK), jnp.bfloat16)
    vmem = pl.BlockSpec(memory_space=pltpu.VMEM)
    rows = HEADS_DEV * BLOCK
    return pl.pallas_call(
        functools.partial(attend_kernel, start, len(parts), state is None, last),
        out_shape=out,
        in_specs=[pl.BlockSpec(memory_space=pltpu.SMEM)] + [vmem] * (len(operands) - 1),
        out_specs=vmem if last else (vmem,) * 3,
        scratch_shapes=[
            pltpu.VMEM((n_keys, 2 * BLOCK), jnp.float32),
            pltpu.VMEM((KV_RANK, n_keys), jnp.bfloat16),
        ],
        compiler_params=pltpu.CompilerParams(vmem_limit_bytes=VMEM_LIMIT),
        cost_estimate=pl.CostEstimate(
            flops=20000000000,
            bytes_accessed=4 * rows * KV_RANK * 2,
            transcendentals=rows * n_keys,
        ),
        name="attend",
    )(*operands)


def index_kernel(place_ref, query_ref, w_ref, own_ref, other_ref, out_ref, wb_ref, q_ref):
    core = place_ref[0]
    first_row = place_ref[1]
    rows = 16
    for head in range(IDX_HEADS):
        q_ref[head * rows : (head + 1) * rows, :] = query_ref[
            :, head * IDX_DIM : (head + 1) * IDX_DIM
        ]
        wb_ref[head * rows : (head + 1) * rows, :] = jnp.broadcast_to(
            w_ref[:, head : head + 1] * (IDX_DIM ** (-0.5)), (rows, BLOCK)
        )
    row_pos = first_row + lax.broadcasted_iota(jnp.int32, (rows, BLOCK), 0)
    lane = lax.broadcasted_iota(jnp.int32, (rows, BLOCK), 1)

    def chunk(keys_ref, parity, step):
        keys = jnp.concatenate(
            [
                keys_ref[step * 2 + half, :, at * IDX_DIM : (at + 1) * IDX_DIM]
                for half in range(2)
                for at in range(8)
            ],
            axis=0,
        )
        dots = lax.dot_general(
            q_ref[...], keys, (((1,), (1,)), ((), ())), preferred_element_type=jnp.float32
        )
        for half in range(2):
            part = dots[:, half * BLOCK : (half + 1) * BLOCK]
            active = jnp.maximum(part, 0.0) * wb_ref[...]
            summed = jnp.sum(active.reshape(IDX_HEADS, rows, BLOCK), axis=0)
            start = pl.multiple_of(((step * 2 + half) * 2 + parity) * BLOCK, BLOCK)
            out_ref[:, pl.ds(start, BLOCK)] = jnp.where(start + lane <= row_pos, summed, 0.0)

    def one(step, carry):
        chunk(own_ref, core, step)
        chunk(other_ref, 1 - core, step)
        return carry

    lax.fori_loop(0, NBLK // 4, one, 0)


def index_part(place, query, weight, own, other):
    return pl.pallas_call(
        index_kernel,
        out_shape=jax.ShapeDtypeStruct((16, NBLK * BLOCK), jnp.float32),
        in_specs=[pl.BlockSpec(memory_space=pltpu.SMEM)]
        + [pl.BlockSpec(memory_space=pltpu.VMEM)] * 4,
        out_specs=pl.BlockSpec(memory_space=pltpu.VMEM),
        scratch_shapes=[
            pltpu.VMEM((IDX_HEADS * 16, BLOCK), jnp.float32),
            pltpu.VMEM((IDX_HEADS * 16, IDX_DIM), jnp.bfloat16),
        ],
        compiler_params=pltpu.CompilerParams(vmem_limit_bytes=VMEM_LIMIT),
        cost_estimate=pl.CostEstimate(
            flops=1_000_000_000, bytes_accessed=4 << 20, transcendentals=0
        ),
        name="index_scores",
    )(place, query, weight, own, other)


def prepare_kernel(lq_ref, up_ref, q_ref, up_t_ref):
    for head in range(HEADS_DEV):
        pair, half = divmod(head, 2)
        q_ref[pair, half * BLOCK : (half + 1) * BLOCK, :] = lq_ref[:, head * LAT : (head + 1) * LAT]
        up_t_ref[head] = up_ref[head].T


def prepare(latent_query, value_up):
    vmem = pl.BlockSpec(memory_space=pltpu.VMEM)
    shapes = [(HEADS_DEV // 2, 2 * BLOCK, LAT), (HEADS_DEV, V_DIM, KV_RANK)]
    return pl.pallas_call(
        prepare_kernel,
        out_shape=[jax.ShapeDtypeStruct(shape, jnp.bfloat16) for shape in shapes],
        in_specs=[vmem] * 2,
        out_specs=[vmem] * 2,
        compiler_params=pltpu.CompilerParams(vmem_limit_bytes=VMEM_LIMIT),
        cost_estimate=pl.CostEstimate(
            flops=20000000000, bytes_accessed=20000000, transcendentals=0
        ),
        name="prepare",
    )(latent_query, value_up)


def arrange_kernel(z_ref, *refs):
    out_ref = refs[NZ]
    for step in range(NZ):
        out_ref[z_ref[0] ^ step] = refs[step][...]


def arrange(z, near):
    vmem = pl.BlockSpec(memory_space=pltpu.VMEM)
    return pl.pallas_call(
        arrange_kernel,
        out_shape=jax.ShapeDtypeStruct((NZ, PACKED, 1024), jnp.bfloat16),
        in_specs=[pl.BlockSpec(memory_space=pltpu.SMEM)] + [vmem] * NZ,
        out_specs=vmem,
        compiler_params=pltpu.CompilerParams(vmem_limit_bytes=VMEM_LIMIT),
        name="arrange",
    )(z, *near)


def project_kernel(w_ref, own_ref, other_ref, out_ref, values_ref):
    @pl.when(pl.program_id(0) == 0)
    def _():
        values_ref[:, :BLOCK] = own_ref[...]
        values_ref[:, BLOCK:] = other_ref[...]

    terms = lax.dot_general(
        w_ref[...].reshape(NZ * PACKED, 1024),
        values_ref[...],
        (((1,), (0,)), ((), ())),
        preferred_element_type=jnp.float32,
    )
    terms = terms.reshape(NZ, PACKED, 2 * BLOCK)[:, 16:, :].reshape(NZ * COLS, 2 * BLOCK)
    out_ref[0] = terms.astype(jnp.bfloat16)


def project(gathered, own, other):
    values = pl.BlockSpec((HEADS_DEV * V_DIM, BLOCK), lambda i: (0, 0))
    return pl.pallas_call(
        project_kernel,
        out_shape=jax.ShapeDtypeStruct((NY, NZ * COLS, 2 * BLOCK), jnp.bfloat16),
        grid=(NY,),
        in_specs=[pl.BlockSpec((NZ, PACKED, 1024), lambda i: (i, 0, 0)), values, values],
        out_specs=pl.BlockSpec((1, NZ * COLS, 2 * BLOCK), lambda i: (i, 0, 0)),
        scratch_shapes=[pltpu.VMEM((HEADS_DEV * V_DIM, 2 * BLOCK), jnp.bfloat16)],
        compiler_params=pltpu.CompilerParams(vmem_limit_bytes=VMEM_LIMIT),
        name="project",
    )(gathered, own, other)


def swap_core(value):
    return lax.ppermute(value, "c", [(0, 1), (1, 0)])


def spread(value, axis, count):
    wide = jnp.broadcast_to(value[None], (count,) + value.shape)
    return lax.all_to_all(wide, axis, 0, 0)


def body(
    index_query, index_weight, index_key, latent_query, latent, block_lists, value_up, out_weight
):
    y, z, core, x, w = (lax.axis_index(name) for name in ("y", "z", "c", "x", "w"))
    ctx_pos = (y * NZ + z) * NC + core
    head_pos = x * NW + w

    own = lax.dynamic_slice_in_dim(latent, head_pos * 16, 16, 0).reshape(1, NC, ROWS, LAT)
    wide = jnp.broadcast_to(own, (NY * NZ, NC, ROWS, LAT)).reshape(NBLK, ROWS, LAT)

    key_rows = jnp.moveaxis(index_key.reshape(8, 16, IDX_DIM), 0, 1).reshape(16, 1024)
    packed = jnp.concatenate([key_rows, out_weight.T], axis=0)
    near = [packed] + [
        lax.ppermute(packed, "z", [(at, at ^ step) for at in range(NZ)]) for step in range(1, NZ)
    ]
    pool = lax.all_to_all(wide, CTX, 0, 0)
    listed = block_lists[0]
    safe = jnp.maximum(listed, 0)
    both = jnp.concatenate([safe, swap_core(safe)])
    offsets = [
        ((x + step) % NX) * 32 + (w ^ far) * 16 + (core ^ half) * ROWS
        for step, far in ((0, 0), (0, 1), (3, 0), (3, 1), (1, 0), (1, 1), (2, 0), (2, 1))
        for half in range(NC)
    ]
    place = jnp.concatenate([listed, jnp.stack([ctx_pos * BLOCK] + offsets)])
    queries, up_t = prepare(latent_query, value_up)
    near_z = arrange(z.reshape(1), near)
    pool, queries, up_t, both, place, near_z = lax.optimization_barrier(
        (pool, queries, up_t, both, place, near_z)
    )
    gathered = lax.all_gather(near_z, "y", axis=0, tiled=True)

    picked = jnp.take(pool, both, axis=0, mode="clip").reshape(2, TOPK * ROWS, LAT)
    mine = jnp.concatenate([picked[0], swap_core(picked[1])], axis=0)
    mine = jnp.concatenate([mine, lax.ppermute(mine, "w", [(0, 1), (1, 0)])], axis=0)
    up = [(at, (at + 1) % NX) for at in range(NX)]
    down = [(at, (at - 1) % NX) for at in range(NX)]
    left = lax.ppermute(mine, "x", up)
    right = lax.ppermute(mine, "x", down)

    state = attend(0, place, queries, [mine], None, None)
    left, right, state = lax.optimization_barrier((left, right, state))
    far_a = lax.ppermute(left[:256], "x", up)
    far_b = lax.ppermute(right[256:], "x", down)
    state = attend(4, place, queries, [left, right], state, None)
    far_a, far_b, state = lax.optimization_barrier((far_a, far_b, state))
    values = attend(12, place, queries, [far_a, far_b], state, up_t)

    values, gathered = lax.optimization_barrier((values, gathered))
    terms = project(gathered, values, swap_core(values))
    keys_own = gathered[:, :16]
    first_row = ctx_pos * TOK_DEV + head_pos * 16
    keys_other = swap_core(keys_own)
    index_scores = index_part(
        jnp.stack([core, first_row]), index_query, index_weight, keys_own, keys_other
    )
    shares = lax.all_to_all(terms, HEAD, 0, 0)
    shares, index_scores = lax.optimization_barrier((shares, index_scores))
    summed = jnp.sum(shares.astype(jnp.float32), axis=0).astype(jnp.bfloat16)
    kept = summed[:, :BLOCK].reshape(NZ, COLS, BLOCK)
    other = swap_core(summed[:, BLOCK:]).reshape(NZ, COLS, BLOCK)
    first = jnp.where(core == 0, kept, other)
    second = jnp.where(core == 0, other, kept)
    attn_out = jnp.stack([first, second], axis=1).reshape(NZ * NC * COLS, BLOCK).T

    return index_scores, attn_out


def solution(mesh):
    fine = Mesh(mesh.devices.reshape(NY, NZ, NC, NX, NW), ("y", "z", "c", "x", "w"))
    return jax.shard_map(
        body,
        mesh=fine,
        in_specs=(
            P(CTX + HEAD, None),
            P(CTX + HEAD, None),
            P(CTX, None),
            P(CTX, HEAD),
            P(CTX, None),
            P(CTX, None),
            P(HEAD, None, None),
            P(HEAD, CTX),
        ),
        out_specs=(P(CTX + HEAD, None), P(CTX, HEAD)),
        check_vma=False,
    )
```

```python
import functools

import jax
import jax.numpy as jnp
from jax import lax
from jax.experimental import pallas as pl
from jax.experimental.pallas import tpu as pltpu
from jax.sharding import Mesh
from jax.sharding import PartitionSpec as P

TOK_DEV = 128
HEADS_DEV = 8
KV_RANK = 512
LAT = 576
V_DIM = 128
IDX_HEADS = 32
IDX_DIM = 128
BLOCK = 128
TOPK = 16
NBLK = 64
ROWS = 16
PACKED = 72
COLS = 56
NY, NZ, NC, NX, NW = 8, 4, 2, 4, 2

CTX = ("y", "z", "c")
HEAD = ("x", "w")
LOG2E = 1.4426950408889634
SCORE_SCALE = 192.0 ** (-0.5) * LOG2E
MASKED = -1e30
VMEM_LIMIT = 56 * 1024 * 1024


def attend_kernel(start, count, first, last, *refs):
    place_ref, q_ref = refs[:2]
    kv_refs = refs[2 : 2 + count]
    refs = refs[2 + count :]
    if not first:
        max_in, total_in, sum_in = refs[:3]
        refs = refs[3:]
    if last:
        up_ref, out_ref = refs[:2]
        refs = refs[2:]
    else:
        max_out, total_out, sum_out = refs[:3]
        refs = refs[3:]
    bias_ref, vt_ref = refs
    keys = jnp.concatenate([ref[...] for ref in kv_refs], axis=0)
    n_keys = keys.shape[0]
    vt_ref[...] = keys[:, :KV_RANK].T
    row = lax.broadcasted_iota(jnp.int32, (ROWS, BLOCK), 0)
    query = place_ref[TOPK] + lax.broadcasted_iota(jnp.int32, (ROWS, BLOCK), 1)
    for group in range(n_keys // ROWS):
        part, slot = divmod(group, TOPK)
        entry = place_ref[slot]
        first_key = jnp.where(entry < 0, 2 * NBLK, entry) * BLOCK
        first_key = first_key + place_ref[TOPK + 1 + start + part]
        seen = jnp.where(first_key + row <= query, 0.0, MASKED)
        bias_ref[group * ROWS : (group + 1) * ROWS, :BLOCK] = seen
        bias_ref[group * ROWS : (group + 1) * ROWS, BLOCK:] = seen
    for pair in range(HEADS_DEV // 2):
        scores = lax.dot_general(
            keys, q_ref[pair], (((1,), (1,)), ((), ())), preferred_element_type=jnp.float32
        )
        scores = scores + bias_ref[...]
        row_max = jnp.max(scores, axis=0, keepdims=True)
        if not first:
            row_max = jnp.maximum(row_max, max_in[pair])
            keep = jnp.exp2((max_in[pair] - row_max) * SCORE_SCALE)
        expo = jnp.exp2((scores - row_max) * SCORE_SCALE)
        total = jnp.sum(expo, axis=0, keepdims=True)
        lat_sum = lax.dot_general(
            vt_ref[...],
            expo.astype(jnp.bfloat16),
            (((1,), (0,)), ((), ())),
            preferred_element_type=jnp.float32,
        )
        if not first:
            total = total + total_in[pair] * keep
            lat_sum = lat_sum + sum_in[pair] * keep
        if not last:
            max_out[pair] = row_max
            total_out[pair] = total
            sum_out[pair] = lat_sum
            continue
        lat_out = (lat_sum / total).astype(jnp.bfloat16)
        for half in range(2):
            head = 2 * pair + half
            values = lax.dot_general(
                up_ref[head],
                lat_out[:, half * BLOCK : (half + 1) * BLOCK],
                (((1,), (0,)), ((), ())),
                preferred_element_type=jnp.float32,
            )
            out_ref[head * V_DIM : (head + 1) * V_DIM, :] = values.astype(jnp.bfloat16)


def attend(start, place, queries, parts, state, up_t):
    pairs = HEADS_DEV // 2
    n_keys = sum(part.shape[0] for part in parts)
    stat = jax.ShapeDtypeStruct((pairs, 1, 2 * BLOCK), jnp.float32)
    out = (stat, stat, jax.ShapeDtypeStruct((pairs, KV_RANK, 2 * BLOCK), jnp.float32))
    last = up_t is not None
    operands = [place, queries, *parts, *(state or ())]
    if last:
        operands.append(up_t)
        out = jax.ShapeDtypeStruct((HEADS_DEV * V_DIM, BLOCK), jnp.bfloat16)
    vmem = pl.BlockSpec(memory_space=pltpu.VMEM)
    rows = HEADS_DEV * BLOCK
    return pl.pallas_call(
        functools.partial(attend_kernel, start, len(parts), state is None, last),
        out_shape=out,
        in_specs=[pl.BlockSpec(memory_space=pltpu.SMEM)] + [vmem] * (len(operands) - 1),
        out_specs=vmem if last else (vmem,) * 3,
        scratch_shapes=[
            pltpu.VMEM((n_keys, 2 * BLOCK), jnp.float32),
            pltpu.VMEM((KV_RANK, n_keys), jnp.bfloat16),
        ],
        compiler_params=pltpu.CompilerParams(vmem_limit_bytes=VMEM_LIMIT),
        cost_estimate=pl.CostEstimate(
            flops=20000000000,
            bytes_accessed=4 * rows * KV_RANK * 2,
            transcendentals=rows * n_keys,
        ),
        name="attend",
    )(*operands)


def index_kernel(place_ref, query_ref, w_ref, own_ref, other_ref, out_ref, wb_ref, q_ref):
    core = place_ref[0]
    first_row = place_ref[1]
    rows = 16
    for head in range(IDX_HEADS):
        q_ref[head * rows : (head + 1) * rows, :] = query_ref[
            :, head * IDX_DIM : (head + 1) * IDX_DIM
        ]
        wb_ref[head * rows : (head + 1) * rows, :] = jnp.broadcast_to(
            w_ref[:, head : head + 1] * (IDX_DIM ** (-0.5)), (rows, BLOCK)
        )
    row_pos = first_row + lax.broadcasted_iota(jnp.int32, (rows, BLOCK), 0)
    lane = lax.broadcasted_iota(jnp.int32, (rows, BLOCK), 1)

    def chunk(keys_ref, parity, step):
        keys = jnp.concatenate(
            [
                keys_ref[step * 2 + half, :, at * IDX_DIM : (at + 1) * IDX_DIM]
                for half in range(2)
                for at in range(8)
            ],
            axis=0,
        )
        dots = lax.dot_general(
            q_ref[...], keys, (((1,), (1,)), ((), ())), preferred_element_type=jnp.float32
        )
        for half in range(2):
            part = dots[:, half * BLOCK : (half + 1) * BLOCK]
            active = jnp.maximum(part, 0.0) * wb_ref[...]
            summed = jnp.sum(active.reshape(IDX_HEADS, rows, BLOCK), axis=0)
            start = pl.multiple_of(((step * 2 + half) * 2 + parity) * BLOCK, BLOCK)
            out_ref[:, pl.ds(start, BLOCK)] = jnp.where(start + lane <= row_pos, summed, 0.0)

    def one(step, carry):
        chunk(own_ref, core, step)
        chunk(other_ref, 1 - core, step)
        return carry

    lax.fori_loop(0, NBLK // 4, one, 0)


def index_part(place, query, weight, own, other):
    return pl.pallas_call(
        index_kernel,
        out_shape=jax.ShapeDtypeStruct((16, NBLK * BLOCK), jnp.float32),
        in_specs=[pl.BlockSpec(memory_space=pltpu.SMEM)]
        + [pl.BlockSpec(memory_space=pltpu.VMEM)] * 4,
        out_specs=pl.BlockSpec(memory_space=pltpu.VMEM),
        scratch_shapes=[
            pltpu.VMEM((IDX_HEADS * 16, BLOCK), jnp.float32),
            pltpu.VMEM((IDX_HEADS * 16, IDX_DIM), jnp.bfloat16),
        ],
        compiler_params=pltpu.CompilerParams(vmem_limit_bytes=VMEM_LIMIT),
        cost_estimate=pl.CostEstimate(
            flops=1_000_000_000, bytes_accessed=4 << 20, transcendentals=0
        ),
        name="index_scores",
    )(place, query, weight, own, other)


def prepare_kernel(lq_ref, up_ref, q_ref, up_t_ref):
    for head in range(HEADS_DEV):
        pair, half = divmod(head, 2)
        q_ref[pair, half * BLOCK : (half + 1) * BLOCK, :] = lq_ref[:, head * LAT : (head + 1) * LAT]
        up_t_ref[head] = up_ref[head].T


def prepare(latent_query, value_up):
    vmem = pl.BlockSpec(memory_space=pltpu.VMEM)
    shapes = [(HEADS_DEV // 2, 2 * BLOCK, LAT), (HEADS_DEV, V_DIM, KV_RANK)]
    return pl.pallas_call(
        prepare_kernel,
        out_shape=[jax.ShapeDtypeStruct(shape, jnp.bfloat16) for shape in shapes],
        in_specs=[vmem] * 2,
        out_specs=[vmem] * 2,
        compiler_params=pltpu.CompilerParams(vmem_limit_bytes=VMEM_LIMIT),
        cost_estimate=pl.CostEstimate(
            flops=80000000000, bytes_accessed=209715200, transcendentals=0
        ),
        name="prepare",
    )(latent_query, value_up)


def arrange_kernel(z_ref, *refs):
    out_ref = refs[NZ]
    for step in range(NZ):
        out_ref[z_ref[0] ^ step] = refs[step][...]


def arrange(z, near):
    vmem = pl.BlockSpec(memory_space=pltpu.VMEM)
    return pl.pallas_call(
        arrange_kernel,
        out_shape=jax.ShapeDtypeStruct((NZ, PACKED, 1024), jnp.bfloat16),
        in_specs=[pl.BlockSpec(memory_space=pltpu.SMEM)] + [vmem] * NZ,
        out_specs=vmem,
        compiler_params=pltpu.CompilerParams(vmem_limit_bytes=VMEM_LIMIT),
        name="arrange",
    )(z, *near)


def project_kernel(w_ref, own_ref, other_ref, out_ref, values_ref):
    @pl.when(pl.program_id(0) == 0)
    def _():
        values_ref[:, :BLOCK] = own_ref[...]
        values_ref[:, BLOCK:] = other_ref[...]

    terms = lax.dot_general(
        w_ref[...].reshape(NZ * PACKED, 1024),
        values_ref[...],
        (((1,), (0,)), ((), ())),
        preferred_element_type=jnp.float32,
    )
    terms = terms.reshape(NZ, PACKED, 2 * BLOCK)[:, 16:, :].reshape(NZ * COLS, 2 * BLOCK)
    out_ref[0] = terms.astype(jnp.bfloat16)


def project(gathered, own, other):
    values = pl.BlockSpec((HEADS_DEV * V_DIM, BLOCK), lambda i: (0, 0))
    return pl.pallas_call(
        project_kernel,
        out_shape=jax.ShapeDtypeStruct((NY, NZ * COLS, 2 * BLOCK), jnp.bfloat16),
        grid=(NY,),
        in_specs=[pl.BlockSpec((NZ, PACKED, 1024), lambda i: (i, 0, 0)), values, values],
        out_specs=pl.BlockSpec((1, NZ * COLS, 2 * BLOCK), lambda i: (i, 0, 0)),
        scratch_shapes=[pltpu.VMEM((HEADS_DEV * V_DIM, 2 * BLOCK), jnp.bfloat16)],
        compiler_params=pltpu.CompilerParams(vmem_limit_bytes=VMEM_LIMIT),
        name="project",
    )(gathered, own, other)


def swap_core(value):
    return lax.ppermute(value, "c", [(0, 1), (1, 0)])


def spread(value, axis, count):
    wide = jnp.broadcast_to(value[None], (count,) + value.shape)
    return lax.all_to_all(wide, axis, 0, 0)


def body(
    index_query, index_weight, index_key, latent_query, latent, block_lists, value_up, out_weight
):
    y, z, core, x, w = (lax.axis_index(name) for name in ("y", "z", "c", "x", "w"))
    ctx_pos = (y * NZ + z) * NC + core
    head_pos = x * NW + w

    own = lax.dynamic_slice_in_dim(latent, x * 32, 32, 0).reshape(1, NC, ROWS, LAT)
    wide = jnp.broadcast_to(own, (NY * NZ, NC, ROWS, LAT)).reshape(NBLK, ROWS, LAT)

    key_rows = jnp.moveaxis(index_key.reshape(8, 16, IDX_DIM), 0, 1).reshape(16, 1024)
    packed = jnp.concatenate([key_rows, out_weight.T], axis=0)
    near = [packed] + [
        lax.ppermute(packed, "z", [(at, at ^ step) for at in range(NZ)]) for step in range(1, NZ)
    ]
    pool = lax.all_to_all(wide, CTX, 0, 0)
    listed = block_lists[0]
    safe = jnp.maximum(listed, 0)
    both = jnp.concatenate([safe, swap_core(safe)])
    offsets = [
        ((x + step) % NX) * 32 + (core ^ half) * ROWS
        for step in (0, 3, 1, 2)
        for half in range(NC)
    ]
    place = jnp.concatenate([listed, jnp.stack([ctx_pos * BLOCK] + offsets)])
    queries, up_t = prepare(latent_query, value_up)
    near_z = arrange(z.reshape(1), near)
    gathered = lax.all_gather(near_z, "y", axis=0, tiled=True)
    pool, queries, up_t, both, place = lax.optimization_barrier(
        (pool, queries, up_t, both, place)
    )

    picked = jnp.take(pool, both, axis=0, mode="clip").reshape(2, TOPK * ROWS, LAT)
    mine = jnp.concatenate([picked[0], swap_core(picked[1])], axis=0)
    up = [(at, (at + 1) % NX) for at in range(NX)]
    down = [(at, (at - 1) % NX) for at in range(NX)]
    left = lax.ppermute(mine, "x", up)
    right = lax.ppermute(mine, "x", down)

    state = attend(0, place, queries, [mine], None, None)
    left, right, state = lax.optimization_barrier((left, right, state))
    far_a = lax.ppermute(left[:256], "x", up)
    far_b = lax.ppermute(right[256:], "x", down)
    state = attend(2, place, queries, [left, right], state, None)
    far_a, far_b, state = lax.optimization_barrier((far_a, far_b, state))
    values = attend(6, place, queries, [far_a, far_b], state, up_t)

    values, gathered = lax.optimization_barrier((values, gathered))
    terms = project(gathered, values, swap_core(values))
    keys_own = gathered[:, :16]
    first_row = ctx_pos * TOK_DEV + head_pos * 16
    keys_other = swap_core(keys_own)
    index_scores = index_part(
        jnp.stack([core, first_row]), index_query, index_weight, keys_own, keys_other
    )
    shares = lax.all_to_all(terms, HEAD, 0, 0)
    shares, index_scores = lax.optimization_barrier((shares, index_scores))
    summed = jnp.sum(shares.astype(jnp.float32), axis=0).astype(jnp.bfloat16)
    kept = summed[:, :BLOCK].reshape(NZ, COLS, BLOCK)
    other = swap_core(summed[:, BLOCK:]).reshape(NZ, COLS, BLOCK)
    first = jnp.where(core == 0, kept, other)
    second = jnp.where(core == 0, other, kept)
    attn_out = jnp.stack([first, second], axis=1).reshape(NZ * NC * COLS, BLOCK).T

    return index_scores, attn_out


def solution(mesh):
    fine = Mesh(mesh.devices.reshape(NY, NZ, NC, NX, NW), ("y", "z", "c", "x", "w"))
    return jax.shard_map(
        body,
        mesh=fine,
        in_specs=(
            P(CTX + HEAD, None),
            P(CTX + HEAD, None),
            P(CTX, None),
            P(CTX, HEAD),
            P(CTX, None),
            P(CTX, None),
            P(HEAD, None, None),
            P(HEAD, CTX),
        ),
        out_specs=(P(CTX + HEAD, None), P(CTX, HEAD)),
        check_vma=False,
    )
```

```python
import functools

import jax
import jax.numpy as jnp
from jax import lax
from jax.experimental import pallas as pl
from jax.experimental.pallas import tpu as pltpu
from jax.sharding import Mesh
from jax.sharding import PartitionSpec as P

TOK_DEV = 128
HEADS_DEV = 8
KV_RANK = 512
LAT = 576
V_DIM = 128
IDX_HEADS = 32
IDX_DIM = 128
BLOCK = 128
TOPK = 16
NBLK = 64
ROWS = 16
PACKED = 72
COLS = 56
NY, NZ, NC, NX, NW = 8, 4, 2, 4, 2

CTX = ("y", "z", "c")
HEAD = ("x", "w")
LOG2E = 1.4426950408889634
SCORE_SCALE = 192.0 ** (-0.5) * LOG2E
MASKED = -1e30
VMEM_LIMIT = 56 * 1024 * 1024


def attend_kernel(start, count, first, last, *refs):
    place_ref, q_ref = refs[:2]
    kv_refs = refs[2 : 2 + count]
    refs = refs[2 + count :]
    if not first:
        max_in, total_in, sum_in = refs[:3]
        refs = refs[3:]
    if last:
        up_ref, out_ref = refs[:2]
        refs = refs[2:]
    else:
        max_out, total_out, sum_out = refs[:3]
        refs = refs[3:]
    bias_ref, vt_ref = refs
    keys = jnp.concatenate([ref[...] for ref in kv_refs], axis=0)
    n_keys = keys.shape[0]
    vt_ref[...] = keys[:, :KV_RANK].T
    row = lax.broadcasted_iota(jnp.int32, (ROWS, BLOCK), 0)
    query = place_ref[TOPK] + lax.broadcasted_iota(jnp.int32, (ROWS, BLOCK), 1)
    for group in range(n_keys // ROWS):
        part, slot = divmod(group, TOPK)
        entry = place_ref[slot]
        first_key = jnp.where(entry < 0, 2 * NBLK, entry) * BLOCK
        first_key = first_key + place_ref[TOPK + 1 + start + part]
        seen = jnp.where(first_key + row <= query, 0.0, MASKED)
        bias_ref[group * ROWS : (group + 1) * ROWS, :BLOCK] = seen
        bias_ref[group * ROWS : (group + 1) * ROWS, BLOCK:] = seen
    for pair in range(HEADS_DEV // 2):
        scores = lax.dot_general(
            keys, q_ref[pair], (((1,), (1,)), ((), ())), preferred_element_type=jnp.float32
        )
        scores = scores + bias_ref[...]
        row_max = jnp.max(scores, axis=0, keepdims=True)
        if not first:
            row_max = jnp.maximum(row_max, max_in[pair])
            keep = jnp.exp2((max_in[pair] - row_max) * SCORE_SCALE)
        expo = jnp.exp2((scores - row_max) * SCORE_SCALE)
        total = jnp.sum(expo, axis=0, keepdims=True)
        lat_sum = lax.dot_general(
            vt_ref[...],
            expo.astype(jnp.bfloat16),
            (((1,), (0,)), ((), ())),
            preferred_element_type=jnp.float32,
        )
        if not first:
            total = total + total_in[pair] * keep
            lat_sum = lat_sum + sum_in[pair] * keep
        if not last:
            max_out[pair] = row_max
            total_out[pair] = total
            sum_out[pair] = lat_sum
            continue
        lat_out = (lat_sum / total).astype(jnp.bfloat16)
        for half in range(2):
            head = 2 * pair + half
            values = lax.dot_general(
                up_ref[head],
                lat_out[:, half * BLOCK : (half + 1) * BLOCK],
                (((1,), (0,)), ((), ())),
                preferred_element_type=jnp.float32,
            )
            out_ref[head * V_DIM : (head + 1) * V_DIM, :] = values.astype(jnp.bfloat16)


def attend(start, place, queries, parts, state, up_t):
    pairs = HEADS_DEV // 2
    n_keys = sum(part.shape[0] for part in parts)
    stat = jax.ShapeDtypeStruct((pairs, 1, 2 * BLOCK), jnp.float32)
    out = (stat, stat, jax.ShapeDtypeStruct((pairs, KV_RANK, 2 * BLOCK), jnp.float32))
    last = up_t is not None
    operands = [place, queries, *parts, *(state or ())]
    if last:
        operands.append(up_t)
        out = jax.ShapeDtypeStruct((HEADS_DEV * V_DIM, BLOCK), jnp.bfloat16)
    vmem = pl.BlockSpec(memory_space=pltpu.VMEM)
    rows = HEADS_DEV * BLOCK
    return pl.pallas_call(
        functools.partial(attend_kernel, start, len(parts), state is None, last),
        out_shape=out,
        in_specs=[pl.BlockSpec(memory_space=pltpu.SMEM)] + [vmem] * (len(operands) - 1),
        out_specs=vmem if last else (vmem,) * 3,
        scratch_shapes=[
            pltpu.VMEM((n_keys, 2 * BLOCK), jnp.float32),
            pltpu.VMEM((KV_RANK, n_keys), jnp.bfloat16),
        ],
        compiler_params=pltpu.CompilerParams(vmem_limit_bytes=VMEM_LIMIT),
        cost_estimate=pl.CostEstimate(
            flops=20000000000,
            bytes_accessed=4 * rows * KV_RANK * 2,
            transcendentals=rows * n_keys,
        ),
        name="attend",
    )(*operands)


def index_kernel(place_ref, query_ref, w_ref, own_ref, other_ref, out_ref, wb_ref, q_ref):
    core = place_ref[0]
    first_row = place_ref[1]
    rows = 16
    for head in range(IDX_HEADS):
        q_ref[head * rows : (head + 1) * rows, :] = query_ref[
            :, head * IDX_DIM : (head + 1) * IDX_DIM
        ]
        wb_ref[head * rows : (head + 1) * rows, :] = jnp.broadcast_to(
            w_ref[:, head : head + 1] * (IDX_DIM ** (-0.5)), (rows, BLOCK)
        )
    row_pos = first_row + lax.broadcasted_iota(jnp.int32, (rows, BLOCK), 0)
    lane = lax.broadcasted_iota(jnp.int32, (rows, BLOCK), 1)

    def chunk(keys_ref, parity, step):
        keys = jnp.concatenate(
            [
                keys_ref[step * 2 + half, :, at * IDX_DIM : (at + 1) * IDX_DIM]
                for half in range(2)
                for at in range(8)
            ],
            axis=0,
        )
        dots = lax.dot_general(
            q_ref[...], keys, (((1,), (1,)), ((), ())), preferred_element_type=jnp.float32
        )
        for half in range(2):
            part = dots[:, half * BLOCK : (half + 1) * BLOCK]
            active = jnp.maximum(part, 0.0) * wb_ref[...]
            summed = jnp.sum(active.reshape(IDX_HEADS, rows, BLOCK), axis=0)
            start = pl.multiple_of(((step * 2 + half) * 2 + parity) * BLOCK, BLOCK)
            out_ref[:, pl.ds(start, BLOCK)] = jnp.where(start + lane <= row_pos, summed, 0.0)

    def one(step, carry):
        chunk(own_ref, core, step)
        chunk(other_ref, 1 - core, step)
        return carry

    lax.fori_loop(0, NBLK // 4, one, 0)


def index_part(place, query, weight, own, other):
    return pl.pallas_call(
        index_kernel,
        out_shape=jax.ShapeDtypeStruct((16, NBLK * BLOCK), jnp.float32),
        in_specs=[pl.BlockSpec(memory_space=pltpu.SMEM)]
        + [pl.BlockSpec(memory_space=pltpu.VMEM)] * 4,
        out_specs=pl.BlockSpec(memory_space=pltpu.VMEM),
        scratch_shapes=[
            pltpu.VMEM((IDX_HEADS * 16, BLOCK), jnp.float32),
            pltpu.VMEM((IDX_HEADS * 16, IDX_DIM), jnp.bfloat16),
        ],
        compiler_params=pltpu.CompilerParams(vmem_limit_bytes=VMEM_LIMIT),
        cost_estimate=pl.CostEstimate(
            flops=100_000_000, bytes_accessed=100_000, transcendentals=0
        ),
        name="index_scores",
    )(place, query, weight, own, other)


def prepare_kernel(lq_ref, up_ref, q_ref, up_t_ref):
    for head in range(HEADS_DEV):
        pair, half = divmod(head, 2)
        q_ref[pair, half * BLOCK : (half + 1) * BLOCK, :] = lq_ref[:, head * LAT : (head + 1) * LAT]
        up_t_ref[head] = up_ref[head].T


def prepare(latent_query, value_up):
    vmem = pl.BlockSpec(memory_space=pltpu.VMEM)
    shapes = [(HEADS_DEV // 2, 2 * BLOCK, LAT), (HEADS_DEV, V_DIM, KV_RANK)]
    return pl.pallas_call(
        prepare_kernel,
        out_shape=[jax.ShapeDtypeStruct(shape, jnp.bfloat16) for shape in shapes],
        in_specs=[vmem] * 2,
        out_specs=[vmem] * 2,
        compiler_params=pltpu.CompilerParams(vmem_limit_bytes=VMEM_LIMIT),
        cost_estimate=pl.CostEstimate(
            flops=80000000000, bytes_accessed=209715200, transcendentals=0
        ),
        name="prepare",
    )(latent_query, value_up)


def arrange_kernel(z_ref, *refs):
    out_ref = refs[NZ]
    for step in range(NZ):
        out_ref[z_ref[0] ^ step] = refs[step][...]


def arrange(z, near):
    vmem = pl.BlockSpec(memory_space=pltpu.VMEM)
    return pl.pallas_call(
        arrange_kernel,
        out_shape=jax.ShapeDtypeStruct((NZ, PACKED, 1024), jnp.bfloat16),
        in_specs=[pl.BlockSpec(memory_space=pltpu.SMEM)] + [vmem] * NZ,
        out_specs=vmem,
        compiler_params=pltpu.CompilerParams(vmem_limit_bytes=VMEM_LIMIT),
        name="arrange",
    )(z, *near)


def project_kernel(w_ref, own_ref, other_ref, out_ref, values_ref):
    @pl.when(pl.program_id(0) == 0)
    def _():
        values_ref[:, :BLOCK] = own_ref[...]
        values_ref[:, BLOCK:] = other_ref[...]

    terms = lax.dot_general(
        w_ref[...].reshape(NZ * PACKED, 1024),
        values_ref[...],
        (((1,), (0,)), ((), ())),
        preferred_element_type=jnp.float32,
    )
    terms = terms.reshape(NZ, PACKED, 2 * BLOCK)[:, 16:, :].reshape(NZ * COLS, 2 * BLOCK)
    out_ref[0] = terms.astype(jnp.bfloat16)


def project(gathered, own, other):
    values = pl.BlockSpec((HEADS_DEV * V_DIM, BLOCK), lambda i: (0, 0))
    return pl.pallas_call(
        project_kernel,
        out_shape=jax.ShapeDtypeStruct((NY, NZ * COLS, 2 * BLOCK), jnp.bfloat16),
        grid=(NY,),
        in_specs=[pl.BlockSpec((NZ, PACKED, 1024), lambda i: (i, 0, 0)), values, values],
        out_specs=pl.BlockSpec((1, NZ * COLS, 2 * BLOCK), lambda i: (i, 0, 0)),
        scratch_shapes=[pltpu.VMEM((HEADS_DEV * V_DIM, 2 * BLOCK), jnp.bfloat16)],
        compiler_params=pltpu.CompilerParams(vmem_limit_bytes=VMEM_LIMIT),
        name="project",
    )(gathered, own, other)


def swap_core(value):
    return lax.ppermute(value, "c", [(0, 1), (1, 0)])


def spread(value, axis, count):
    wide = jnp.broadcast_to(value[None], (count,) + value.shape)
    return lax.all_to_all(wide, axis, 0, 0)


def body(
    index_query, index_weight, index_key, latent_query, latent, block_lists, value_up, out_weight
):
    y, z, core, x, w = (lax.axis_index(name) for name in ("y", "z", "c", "x", "w"))
    ctx_pos = (y * NZ + z) * NC + core
    head_pos = x * NW + w

    own = lax.dynamic_slice_in_dim(latent, x * 32, 32, 0).reshape(1, NC, ROWS, LAT)
    wide = jnp.broadcast_to(own, (NY * NZ, NC, ROWS, LAT)).reshape(NBLK, ROWS, LAT)

    key_rows = jnp.moveaxis(index_key.reshape(8, 16, IDX_DIM), 0, 1).reshape(16, 1024)
    packed = jnp.concatenate([key_rows, out_weight.T], axis=0)
    near = [packed] + [
        lax.ppermute(packed, "z", [(at, at ^ step) for at in range(NZ)]) for step in range(1, NZ)
    ]
    pool = lax.all_to_all(wide, CTX, 0, 0)
    listed = block_lists[0]
    safe = jnp.maximum(listed, 0)
    both = jnp.concatenate([safe, swap_core(safe)])
    offsets = [
        ((x + step) % NX) * 32 + (core ^ half) * ROWS
        for step in (0, 3, 1, 2)
        for half in range(NC)
    ]
    place = jnp.concatenate([listed, jnp.stack([ctx_pos * BLOCK] + offsets)])
    queries, up_t = prepare(latent_query, value_up)
    near_z = arrange(z.reshape(1), near)
    gathered = lax.all_gather(near_z, "y", axis=0, tiled=True)
    pool, queries, up_t, both, place = lax.optimization_barrier(
        (pool, queries, up_t, both, place)
    )

    picked = jnp.take(pool, both, axis=0, mode="clip").reshape(2, TOPK * ROWS, LAT)
    mine = jnp.concatenate([picked[0], swap_core(picked[1])], axis=0)
    up = [(at, (at + 1) % NX) for at in range(NX)]
    down = [(at, (at - 1) % NX) for at in range(NX)]
    left = lax.ppermute(mine, "x", up)
    right = lax.ppermute(mine, "x", down)

    state = attend(0, place, queries, [mine], None, None)
    left, right, state = lax.optimization_barrier((left, right, state))
    far_a = lax.ppermute(left[:256], "x", up)
    far_b = lax.ppermute(right[256:], "x", down)
    state = attend(2, place, queries, [left, right], state, None)
    far_a, far_b, state = lax.optimization_barrier((far_a, far_b, state))
    values = attend(6, place, queries, [far_a, far_b], state, up_t)

    values, gathered = lax.optimization_barrier((values, gathered))
    terms = project(gathered, values, swap_core(values))
    terms, gathered = lax.optimization_barrier((terms, gathered))
    keys_own = gathered[:, :16]
    keys_other = swap_core(keys_own)
    shares = lax.all_to_all(terms.reshape(NX, NW, NZ * COLS, 2 * BLOCK), "x", 0, 0)
    first_row = ctx_pos * TOK_DEV + head_pos * 16
    index_scores = index_part(
        jnp.stack([core, first_row]), index_query, index_weight, keys_own, keys_other
    )
    shares, index_scores = lax.optimization_barrier((shares, index_scores))
    summed = jnp.sum(shares.astype(jnp.float32), axis=0)
    sent = jnp.where(w == 0, summed[1], summed[0]).astype(jnp.bfloat16)
    kept = jnp.where(w == 0, summed[0], summed[1])
    came = lax.ppermute(sent, "w", [(0, 1), (1, 0)])
    summed = (kept + came.astype(jnp.float32)).astype(jnp.bfloat16)
    kept = summed[:, :BLOCK].reshape(NZ, COLS, BLOCK)
    other = swap_core(summed[:, BLOCK:]).reshape(NZ, COLS, BLOCK)
    first = jnp.where(core == 0, kept, other)
    second = jnp.where(core == 0, other, kept)
    attn_out = jnp.stack([first, second], axis=1).reshape(NZ * NC * COLS, BLOCK).T

    return index_scores, attn_out


def solution(mesh):
    fine = Mesh(mesh.devices.reshape(NY, NZ, NC, NX, NW), ("y", "z", "c", "x", "w"))
    return jax.shard_map(
        body,
        mesh=fine,
        in_specs=(
            P(CTX + HEAD, None),
            P(CTX + HEAD, None),
            P(CTX, None),
            P(CTX, HEAD),
            P(CTX, None),
            P(CTX, None),
            P(HEAD, None, None),
            P(HEAD, CTX),
        ),
        out_specs=(P(CTX + HEAD, None), P(CTX, HEAD)),
        check_vma=False,
    )
```

```python
import functools

import jax
import jax.numpy as jnp
from jax import lax
from jax.experimental import pallas as pl
from jax.experimental.pallas import tpu as pltpu
from jax.sharding import Mesh
from jax.sharding import PartitionSpec as P

TOK_DEV = 128
HEADS_DEV = 8
KV_RANK = 512
LAT = 576
V_DIM = 128
IDX_HEADS = 32
IDX_DIM = 128
BLOCK = 128
TOPK = 16
NBLK = 64
ROWS = 16
PACKED = 72
SHARED = 8
STEPS = 2
COLS = 56
NY, NZ, NC, NX, NW = 8, 4, 2, 4, 2

CTX = ("y", "z", "c")
HEAD = ("x", "w")
LOG2E = 1.4426950408889634
SCORE_SCALE = 192.0 ** (-0.5) * LOG2E
MASKED = -1e30
VMEM_LIMIT = 56 * 1024 * 1024


def attend_kernel(start, count, first, last, *refs):
    place_ref, q_ref = refs[:2]
    kv_refs = refs[2 : 2 + count]
    refs = refs[2 + count :]
    if not first:
        max_in, total_in, sum_in = refs[:3]
        refs = refs[3:]
    if last:
        up_ref, out_ref = refs[:2]
        refs = refs[2:]
    else:
        max_out, total_out, sum_out = refs[:3]
        refs = refs[3:]
    bias_ref, vt_ref = refs
    keys = jnp.concatenate([ref[...] for ref in kv_refs], axis=0)
    n_keys = keys.shape[0]
    vt_ref[...] = keys[:, :KV_RANK].T
    row = lax.broadcasted_iota(jnp.int32, (ROWS, BLOCK), 0)
    query = place_ref[TOPK] + lax.broadcasted_iota(jnp.int32, (ROWS, BLOCK), 1)
    for group in range(n_keys // ROWS):
        part, slot = divmod(group, TOPK)
        entry = place_ref[slot]
        first_key = jnp.where(entry < 0, 2 * NBLK, entry) * BLOCK
        first_key = first_key + place_ref[TOPK + 1 + start + part]
        seen = jnp.where(first_key + row <= query, 0.0, MASKED)
        bias_ref[group * ROWS : (group + 1) * ROWS, :] = jnp.concatenate([seen] * SHARED, axis=1)
    for pair in range(HEADS_DEV // SHARED):
        scores = lax.dot_general(
            keys, q_ref[pair], (((1,), (1,)), ((), ())), preferred_element_type=jnp.float32
        )
        scores = scores + bias_ref[...]
        row_max = jnp.max(scores, axis=0, keepdims=True)
        if not first:
            row_max = jnp.maximum(row_max, max_in[pair])
            keep = jnp.exp2((max_in[pair] - row_max) * SCORE_SCALE)
        expo = jnp.exp2((scores - row_max) * SCORE_SCALE)
        total = jnp.sum(expo, axis=0, keepdims=True)
        lat_sum = lax.dot_general(
            vt_ref[...],
            expo.astype(jnp.bfloat16),
            (((1,), (0,)), ((), ())),
            preferred_element_type=jnp.float32,
        )
        if not first:
            total = total + total_in[pair] * keep
            lat_sum = lat_sum + sum_in[pair] * keep
        if not last:
            max_out[pair] = row_max
            total_out[pair] = total
            sum_out[pair] = lat_sum
            continue
        lat_out = (lat_sum / total).astype(jnp.bfloat16)
        for half in range(SHARED):
            head = SHARED * pair + half
            values = lax.dot_general(
                up_ref[head],
                lat_out[:, half * BLOCK : (half + 1) * BLOCK],
                (((1,), (0,)), ((), ())),
                preferred_element_type=jnp.float32,
            )
            out_ref[head * V_DIM : (head + 1) * V_DIM, :] = values.astype(jnp.bfloat16)


def attend(start, place, queries, parts, state, up_t):
    pairs = HEADS_DEV // SHARED
    n_keys = sum(part.shape[0] for part in parts)
    stat = jax.ShapeDtypeStruct((pairs, 1, SHARED * BLOCK), jnp.float32)
    out = (stat, stat, jax.ShapeDtypeStruct((pairs, KV_RANK, SHARED * BLOCK), jnp.float32))
    last = up_t is not None
    operands = [place, queries, *parts, *(state or ())]
    if last:
        operands.append(up_t)
        out = jax.ShapeDtypeStruct((HEADS_DEV * V_DIM, BLOCK), jnp.bfloat16)
    vmem = pl.BlockSpec(memory_space=pltpu.VMEM)
    rows = HEADS_DEV * BLOCK
    return pl.pallas_call(
        functools.partial(attend_kernel, start, len(parts), state is None, last),
        out_shape=out,
        in_specs=[pl.BlockSpec(memory_space=pltpu.SMEM)] + [vmem] * (len(operands) - 1),
        out_specs=vmem if last else (vmem,) * 3,
        scratch_shapes=[
            pltpu.VMEM((n_keys, SHARED * BLOCK), jnp.float32),
            pltpu.VMEM((KV_RANK, n_keys), jnp.bfloat16),
        ],
        compiler_params=pltpu.CompilerParams(vmem_limit_bytes=VMEM_LIMIT),
        cost_estimate=pl.CostEstimate(
            flops=20000000000,
            bytes_accessed=4 * rows * KV_RANK * 2,
            transcendentals=rows * n_keys,
        ),
        name="attend",
    )(*operands)


def index_kernel(place_ref, query_ref, w_ref, own_ref, other_ref, out_ref, wb_ref, q_ref):
    core = place_ref[0]
    first_row = place_ref[1]
    rows = 16
    for head in range(IDX_HEADS):
        q_ref[head * rows : (head + 1) * rows, :] = query_ref[
            :, head * IDX_DIM : (head + 1) * IDX_DIM
        ]
        wb_ref[head * rows : (head + 1) * rows, :] = jnp.broadcast_to(
            w_ref[:, head : head + 1] * (IDX_DIM ** (-0.5)), (rows, BLOCK)
        )
    row_pos = first_row + lax.broadcasted_iota(jnp.int32, (rows, BLOCK), 0)
    lane = lax.broadcasted_iota(jnp.int32, (rows, BLOCK), 1)

    def chunk(keys_ref, parity, step):
        keys = jnp.concatenate(
            [
                keys_ref[step * 2 + half, :, at * IDX_DIM : (at + 1) * IDX_DIM]
                for half in range(2)
                for at in range(8)
            ],
            axis=0,
        )
        dots = lax.dot_general(
            q_ref[...], keys, (((1,), (1,)), ((), ())), preferred_element_type=jnp.float32
        )
        for half in range(2):
            part = dots[:, half * BLOCK : (half + 1) * BLOCK]
            active = jnp.maximum(part, 0.0) * wb_ref[...]
            summed = jnp.sum(active.reshape(IDX_HEADS, rows, BLOCK), axis=0)
            start = pl.multiple_of(((step * 2 + half) * 2 + parity) * BLOCK, BLOCK)
            out_ref[:, pl.ds(start, BLOCK)] = jnp.where(start + lane <= row_pos, summed, 0.0)

    def one(step, carry):
        chunk(own_ref, core, step)
        chunk(other_ref, 1 - core, step)
        return carry

    lax.fori_loop(0, NBLK // 4, one, 0)


def index_part(place, query, weight, own, other):
    return pl.pallas_call(
        index_kernel,
        out_shape=jax.ShapeDtypeStruct((16, NBLK * BLOCK), jnp.float32),
        in_specs=[pl.BlockSpec(memory_space=pltpu.SMEM)]
        + [pl.BlockSpec(memory_space=pltpu.VMEM)] * 4,
        out_specs=pl.BlockSpec(memory_space=pltpu.VMEM),
        scratch_shapes=[
            pltpu.VMEM((IDX_HEADS * 16, BLOCK), jnp.float32),
            pltpu.VMEM((IDX_HEADS * 16, IDX_DIM), jnp.bfloat16),
        ],
        compiler_params=pltpu.CompilerParams(vmem_limit_bytes=VMEM_LIMIT),
        cost_estimate=pl.CostEstimate(
            flops=100_000_000, bytes_accessed=100_000, transcendentals=0
        ),
        name="index_scores",
    )(place, query, weight, own, other)


def prepare_kernel(lq_ref, up_ref, q_ref, up_t_ref):
    for head in range(HEADS_DEV):
        pair, half = divmod(head, SHARED)
        q_ref[pair, half * BLOCK : (half + 1) * BLOCK, :] = lq_ref[:, head * LAT : (head + 1) * LAT]
        up_t_ref[head] = up_ref[head].T


def prepare(latent_query, value_up):
    vmem = pl.BlockSpec(memory_space=pltpu.VMEM)
    shapes = [(HEADS_DEV // SHARED, SHARED * BLOCK, LAT), (HEADS_DEV, V_DIM, KV_RANK)]
    return pl.pallas_call(
        prepare_kernel,
        out_shape=[jax.ShapeDtypeStruct(shape, jnp.bfloat16) for shape in shapes],
        in_specs=[vmem] * 2,
        out_specs=[vmem] * 2,
        compiler_params=pltpu.CompilerParams(vmem_limit_bytes=VMEM_LIMIT),
        cost_estimate=pl.CostEstimate(
            flops=80000000000, bytes_accessed=209715200, transcendentals=0
        ),
        name="prepare",
    )(latent_query, value_up)


def arrange_kernel(z_ref, *refs):
    out_ref = refs[NZ]
    for step in range(NZ):
        out_ref[z_ref[0] ^ step] = refs[step][...]


def arrange(z, near):
    vmem = pl.BlockSpec(memory_space=pltpu.VMEM)
    return pl.pallas_call(
        arrange_kernel,
        out_shape=jax.ShapeDtypeStruct((NZ, PACKED, 1024), jnp.bfloat16),
        in_specs=[pl.BlockSpec(memory_space=pltpu.SMEM)] + [vmem] * NZ,
        out_specs=vmem,
        compiler_params=pltpu.CompilerParams(vmem_limit_bytes=VMEM_LIMIT),
        name="arrange",
    )(z, *near)


def project_kernel(w_ref, own_ref, other_ref, out_ref, values_ref):
    @pl.when(pl.program_id(0) == 0)
    def _():
        values_ref[:, :BLOCK] = own_ref[...]
        values_ref[:, BLOCK:] = other_ref[...]

    terms = lax.dot_general(
        w_ref[...].reshape(NY * NZ * PACKED // STEPS, 1024),
        values_ref[...],
        (((1,), (0,)), ((), ())),
        preferred_element_type=jnp.float32,
    )
    terms = terms.reshape(NY * NZ // STEPS, PACKED, 2 * BLOCK)[:, 16:, :]
    out_ref[...] = terms.reshape(NY // STEPS, NZ * COLS, 2 * BLOCK).astype(jnp.bfloat16)


def project(gathered, own, other):
    values = pl.BlockSpec((HEADS_DEV * V_DIM, BLOCK), lambda i: (0, 0))
    return pl.pallas_call(
        project_kernel,
        out_shape=jax.ShapeDtypeStruct((NY, NZ * COLS, 2 * BLOCK), jnp.bfloat16),
        grid=(STEPS,),
        in_specs=[pl.BlockSpec((NY * NZ // STEPS, PACKED, 1024), lambda i: (i, 0, 0)), values, values],
        out_specs=pl.BlockSpec((NY // STEPS, NZ * COLS, 2 * BLOCK), lambda i: (i, 0, 0)),
        scratch_shapes=[pltpu.VMEM((HEADS_DEV * V_DIM, 2 * BLOCK), jnp.bfloat16)],
        compiler_params=pltpu.CompilerParams(vmem_limit_bytes=VMEM_LIMIT),
        name="project",
    )(gathered, own, other)


def swap_core(value):
    return lax.ppermute(value, "c", [(0, 1), (1, 0)])


def spread(value, axis, count):
    wide = jnp.broadcast_to(value[None], (count,) + value.shape)
    return lax.all_to_all(wide, axis, 0, 0)


def body(
    index_query, index_weight, index_key, latent_query, latent, block_lists, value_up, out_weight
):
    y, z, core, x, w = (lax.axis_index(name) for name in ("y", "z", "c", "x", "w"))
    ctx_pos = (y * NZ + z) * NC + core
    head_pos = x * NW + w

    own = lax.dynamic_slice_in_dim(latent, x * 32, 32, 0).reshape(1, NC, ROWS, LAT)
    wide = jnp.broadcast_to(own, (NY * NZ, NC, ROWS, LAT)).reshape(NBLK, ROWS, LAT)

    key_rows = jnp.moveaxis(index_key.reshape(8, 16, IDX_DIM), 0, 1).reshape(16, 1024)
    packed = jnp.concatenate([key_rows, out_weight.T], axis=0)
    near = [packed] + [
        lax.ppermute(packed, "z", [(at, at ^ step) for at in range(NZ)]) for step in range(1, NZ)
    ]
    pool = lax.all_to_all(wide, CTX, 0, 0)
    listed = block_lists[0]
    safe = jnp.maximum(listed, 0)
    both = jnp.concatenate([safe, swap_core(safe)])
    offsets = [
        ((x + step) % NX) * 32 + (core ^ half) * ROWS
        for step in (0, 3, 1, 2)
        for half in range(NC)
    ]
    place = jnp.concatenate([listed, jnp.stack([ctx_pos * BLOCK] + offsets)])
    queries, up_t = prepare(latent_query, value_up)
    near_z = arrange(z.reshape(1), near)
    gathered = lax.all_gather(near_z, "y", axis=0, tiled=True)
    pool, queries, up_t, both, place = lax.optimization_barrier(
        (pool, queries, up_t, both, place)
    )

    picked = jnp.take(pool, both, axis=0, mode="clip").reshape(2, TOPK * ROWS, LAT)
    mine = jnp.concatenate([picked[0], swap_core(picked[1])], axis=0)
    up = [(at, (at + 1) % NX) for at in range(NX)]
    down = [(at, (at - 1) % NX) for at in range(NX)]
    left = lax.ppermute(mine, "x", up)
    right = lax.ppermute(mine, "x", down)

    state = attend(0, place, queries, [mine], None, None)
    left, right, state = lax.optimization_barrier((left, right, state))
    far_a = lax.ppermute(left[:256], "x", up)
    far_b = lax.ppermute(right[256:], "x", down)
    state = attend(2, place, queries, [left, right], state, None)
    far_a, far_b, state = lax.optimization_barrier((far_a, far_b, state))
    values = attend(6, place, queries, [far_a, far_b], state, up_t)

    values, gathered = lax.optimization_barrier((values, gathered))
    terms = project(gathered, values, swap_core(values))
    terms, gathered = lax.optimization_barrier((terms, gathered))
    keys_own = gathered[:, :16]
    keys_other = swap_core(keys_own)
    shares = lax.all_to_all(terms.reshape(NX, NW, NZ * COLS, 2 * BLOCK), "x", 0, 0)
    first_row = ctx_pos * TOK_DEV + head_pos * 16
    index_scores = index_part(
        jnp.stack([core, first_row]), index_query, index_weight, keys_own, keys_other
    )
    shares, index_scores = lax.optimization_barrier((shares, index_scores))
    summed = jnp.sum(shares.astype(jnp.float32), axis=0)
    sent = jnp.where(w == 0, summed[1], summed[0]).astype(jnp.bfloat16)
    kept = jnp.where(w == 0, summed[0], summed[1])
    came = lax.ppermute(sent, "w", [(0, 1), (1, 0)])
    summed = (kept + came.astype(jnp.float32)).astype(jnp.bfloat16)
    kept = summed[:, :BLOCK].reshape(NZ, COLS, BLOCK)
    other = swap_core(summed[:, BLOCK:]).reshape(NZ, COLS, BLOCK)
    first = jnp.where(core == 0, kept, other)
    second = jnp.where(core == 0, other, kept)
    attn_out = jnp.stack([first, second], axis=1).reshape(NZ * NC * COLS, BLOCK).T

    return index_scores, attn_out


def solution(mesh):
    fine = Mesh(mesh.devices.reshape(NY, NZ, NC, NX, NW), ("y", "z", "c", "x", "w"))
    return jax.shard_map(
        body,
        mesh=fine,
        in_specs=(
            P(CTX + HEAD, None),
            P(CTX + HEAD, None),
            P(CTX, None),
            P(CTX, HEAD),
            P(CTX, None),
            P(CTX, None),
            P(HEAD, None, None),
            P(HEAD, CTX),
        ),
        out_specs=(P(CTX + HEAD, None), P(CTX, HEAD)),
        check_vma=False,
    )
```

```python
import functools

import jax
import jax.numpy as jnp
from jax import lax
from jax.experimental import pallas as pl
from jax.experimental.pallas import tpu as pltpu
from jax.sharding import Mesh
from jax.sharding import PartitionSpec as P

TOK_DEV = 128
HEADS_DEV = 8
KV_RANK = 512
LAT = 576
V_DIM = 128
IDX_HEADS = 32
IDX_DIM = 128
BLOCK = 128
TOPK = 16
NBLK = 64
ROWS = 16
PACKED = 72
SHARED = 8
STEPS = 2
COLS = 56
NY, NZ, NC, NX, NW = 8, 4, 2, 4, 2

CTX = ("y", "z", "c")
HEAD = ("x", "w")
LOG2E = 1.4426950408889634
SCORE_SCALE = 192.0 ** (-0.5) * LOG2E
MASKED = -1e30
VMEM_LIMIT = 56 * 1024 * 1024


def attend_kernel(start, count, first, last, *refs):
    place_ref, q_ref = refs[:2]
    kv_refs = refs[2 : 2 + count]
    refs = refs[2 + count :]
    if not first:
        max_in, total_in, sum_in = refs[:3]
        refs = refs[3:]
    if last:
        up_ref, out_ref = refs[:2]
        refs = refs[2:]
    else:
        max_out, total_out, sum_out = refs[:3]
        refs = refs[3:]
    bias_ref, vt_ref = refs
    keys = jnp.concatenate([ref[...] for ref in kv_refs], axis=0)
    n_keys = keys.shape[0]
    vt_ref[...] = keys[:, :KV_RANK].T
    row = lax.broadcasted_iota(jnp.int32, (ROWS, BLOCK), 0)
    query = place_ref[TOPK] + lax.broadcasted_iota(jnp.int32, (ROWS, BLOCK), 1)
    for group in range(n_keys // ROWS):
        part, slot = divmod(group, TOPK)
        entry = place_ref[slot]
        first_key = jnp.where(entry < 0, 2 * NBLK, entry) * BLOCK
        first_key = first_key + place_ref[TOPK + 1 + start + part]
        seen = jnp.where(first_key + row <= query, 0.0, MASKED)
        bias_ref[group * ROWS : (group + 1) * ROWS, :] = jnp.concatenate([seen] * SHARED, axis=1)
    for pair in range(HEADS_DEV // SHARED):
        scores = lax.dot_general(
            keys, q_ref[pair], (((1,), (1,)), ((), ())), preferred_element_type=jnp.float32
        )
        scores = scores + bias_ref[...]
        row_max = jnp.max(scores, axis=0, keepdims=True)
        if not first:
            row_max = jnp.maximum(row_max, max_in[pair])
            keep = jnp.exp2((max_in[pair] - row_max) * SCORE_SCALE)
        expo = jnp.exp2((scores - row_max) * SCORE_SCALE)
        total = jnp.sum(expo, axis=0, keepdims=True)
        lat_sum = lax.dot_general(
            vt_ref[...],
            expo.astype(jnp.bfloat16),
            (((1,), (0,)), ((), ())),
            preferred_element_type=jnp.float32,
        )
        if not first:
            total = total + total_in[pair] * keep
            lat_sum = lat_sum + sum_in[pair] * keep
        if not last:
            max_out[pair] = row_max
            total_out[pair] = total
            sum_out[pair] = lat_sum
            continue
        lat_out = (lat_sum / total).astype(jnp.bfloat16)
        for half in range(SHARED):
            head = SHARED * pair + half
            values = lax.dot_general(
                up_ref[head],
                lat_out[:, half * BLOCK : (half + 1) * BLOCK],
                (((1,), (0,)), ((), ())),
                preferred_element_type=jnp.float32,
            )
            out_ref[head * V_DIM : (head + 1) * V_DIM, :] = values.astype(jnp.bfloat16)


def attend(start, place, queries, parts, state, up_t):
    pairs = HEADS_DEV // SHARED
    n_keys = sum(part.shape[0] for part in parts)
    stat = jax.ShapeDtypeStruct((pairs, 1, SHARED * BLOCK), jnp.float32)
    out = (stat, stat, jax.ShapeDtypeStruct((pairs, KV_RANK, SHARED * BLOCK), jnp.float32))
    last = up_t is not None
    operands = [place, queries, *parts, *(state or ())]
    if last:
        operands.append(up_t)
        out = jax.ShapeDtypeStruct((HEADS_DEV * V_DIM, BLOCK), jnp.bfloat16)
    vmem = pl.BlockSpec(memory_space=pltpu.VMEM)
    rows = HEADS_DEV * BLOCK
    return pl.pallas_call(
        functools.partial(attend_kernel, start, len(parts), state is None, last),
        out_shape=out,
        in_specs=[pl.BlockSpec(memory_space=pltpu.SMEM)] + [vmem] * (len(operands) - 1),
        out_specs=vmem if last else (vmem,) * 3,
        scratch_shapes=[
            pltpu.VMEM((n_keys, SHARED * BLOCK), jnp.float32),
            pltpu.VMEM((KV_RANK, n_keys), jnp.bfloat16),
        ],
        compiler_params=pltpu.CompilerParams(vmem_limit_bytes=VMEM_LIMIT),
        cost_estimate=pl.CostEstimate(
            flops=20000000000,
            bytes_accessed=4 * rows * KV_RANK * 2,
            transcendentals=rows * n_keys,
        ),
        name="attend",
    )(*operands)


def index_kernel(place_ref, query_ref, w_ref, own_ref, other_ref, out_ref, wb_ref, q_ref):
    core = place_ref[0]
    first_row = place_ref[1]
    rows = 16
    for head in range(IDX_HEADS):
        q_ref[head * rows : (head + 1) * rows, :] = query_ref[
            :, head * IDX_DIM : (head + 1) * IDX_DIM
        ]
        wb_ref[head * rows : (head + 1) * rows, :] = jnp.broadcast_to(
            w_ref[:, head : head + 1] * (IDX_DIM ** (-0.5)), (rows, BLOCK)
        )
    row_pos = first_row + lax.broadcasted_iota(jnp.int32, (rows, BLOCK), 0)
    lane = lax.broadcasted_iota(jnp.int32, (rows, BLOCK), 1)

    def chunk(keys_ref, parity, step):
        keys = jnp.concatenate(
            [
                keys_ref[step * 2 + half, :, at * IDX_DIM : (at + 1) * IDX_DIM]
                for half in range(2)
                for at in range(8)
            ],
            axis=0,
        )
        dots = lax.dot_general(
            q_ref[...], keys, (((1,), (1,)), ((), ())), preferred_element_type=jnp.float32
        )
        for half in range(2):
            part = dots[:, half * BLOCK : (half + 1) * BLOCK]
            active = jnp.maximum(part, 0.0) * wb_ref[...]
            summed = jnp.sum(active.reshape(IDX_HEADS, rows, BLOCK), axis=0)
            start = pl.multiple_of(((step * 2 + half) * 2 + parity) * BLOCK, BLOCK)
            out_ref[:, pl.ds(start, BLOCK)] = jnp.where(start + lane <= row_pos, summed, 0.0)

    def one(step, carry):
        chunk(own_ref, core, step)
        chunk(other_ref, 1 - core, step)
        return carry

    lax.fori_loop(0, NBLK // 4, one, 0)


def index_part(place, query, weight, own, other):
    return pl.pallas_call(
        index_kernel,
        out_shape=jax.ShapeDtypeStruct((16, NBLK * BLOCK), jnp.float32),
        in_specs=[pl.BlockSpec(memory_space=pltpu.SMEM)]
        + [pl.BlockSpec(memory_space=pltpu.VMEM)] * 4,
        out_specs=pl.BlockSpec(memory_space=pltpu.VMEM),
        scratch_shapes=[
            pltpu.VMEM((IDX_HEADS * 16, BLOCK), jnp.float32),
            pltpu.VMEM((IDX_HEADS * 16, IDX_DIM), jnp.bfloat16),
        ],
        compiler_params=pltpu.CompilerParams(vmem_limit_bytes=VMEM_LIMIT),
        cost_estimate=pl.CostEstimate(
            flops=100_000_000, bytes_accessed=100_000, transcendentals=0
        ),
        name="index_scores",
    )(place, query, weight, own, other)


def prepare_kernel(lq_ref, up_ref, q_ref, up_t_ref):
    for head in range(HEADS_DEV):
        pair, half = divmod(head, SHARED)
        q_ref[pair, half * BLOCK : (half + 1) * BLOCK, :] = lq_ref[:, head * LAT : (head + 1) * LAT]
        up_t_ref[head] = up_ref[head].T


def prepare(latent_query, value_up):
    vmem = pl.BlockSpec(memory_space=pltpu.VMEM)
    shapes = [(HEADS_DEV // SHARED, SHARED * BLOCK, LAT), (HEADS_DEV, V_DIM, KV_RANK)]
    return pl.pallas_call(
        prepare_kernel,
        out_shape=[jax.ShapeDtypeStruct(shape, jnp.bfloat16) for shape in shapes],
        in_specs=[vmem] * 2,
        out_specs=[vmem] * 2,
        compiler_params=pltpu.CompilerParams(vmem_limit_bytes=VMEM_LIMIT),
        cost_estimate=pl.CostEstimate(
            flops=1000000000, bytes_accessed=4000000, transcendentals=0
        ),
        name="prepare",
    )(latent_query, value_up)


def arrange_kernel(z_ref, pair_ref, across_ref, out_ref):
    for step in range(2):
        out_ref[z_ref[0] ^ step] = pair_ref[step]
        out_ref[z_ref[0] ^ 2 ^ step] = across_ref[step]


def arrange(z, pair, across):
    vmem = pl.BlockSpec(memory_space=pltpu.VMEM)
    return pl.pallas_call(
        arrange_kernel,
        out_shape=jax.ShapeDtypeStruct((NZ, PACKED, 1024), jnp.bfloat16),
        in_specs=[pl.BlockSpec(memory_space=pltpu.SMEM)] + [vmem] * 2,
        out_specs=vmem,
        compiler_params=pltpu.CompilerParams(vmem_limit_bytes=VMEM_LIMIT),
        name="arrange",
    )(z, pair, across)


def project_kernel(w_ref, own_ref, other_ref, out_ref, values_ref):
    @pl.when(pl.program_id(0) == 0)
    def _():
        values_ref[:, :BLOCK] = own_ref[...]
        values_ref[:, BLOCK:] = other_ref[...]

    terms = lax.dot_general(
        w_ref[...].reshape(NY * NZ * PACKED // STEPS, 1024),
        values_ref[...],
        (((1,), (0,)), ((), ())),
        preferred_element_type=jnp.float32,
    )
    terms = terms.reshape(NY * NZ // STEPS, PACKED, 2 * BLOCK)[:, 16:, :]
    out_ref[...] = terms.reshape(NY // STEPS, NZ * COLS, 2 * BLOCK).astype(jnp.bfloat16)


def project(gathered, own, other):
    values = pl.BlockSpec((HEADS_DEV * V_DIM, BLOCK), lambda i: (0, 0))
    return pl.pallas_call(
        project_kernel,
        out_shape=jax.ShapeDtypeStruct((NY, NZ * COLS, 2 * BLOCK), jnp.bfloat16),
        grid=(STEPS,),
        in_specs=[pl.BlockSpec((NY * NZ // STEPS, PACKED, 1024), lambda i: (i, 0, 0)), values, values],
        out_specs=pl.BlockSpec((NY // STEPS, NZ * COLS, 2 * BLOCK), lambda i: (i, 0, 0)),
        scratch_shapes=[pltpu.VMEM((HEADS_DEV * V_DIM, 2 * BLOCK), jnp.bfloat16)],
        compiler_params=pltpu.CompilerParams(vmem_limit_bytes=VMEM_LIMIT),
        name="project",
    )(gathered, own, other)


def swap_core(value):
    return lax.ppermute(value, "c", [(0, 1), (1, 0)])


def spread(value, axis, count):
    wide = jnp.broadcast_to(value[None], (count,) + value.shape)
    return lax.all_to_all(wide, axis, 0, 0)


def body(
    index_query, index_weight, index_key, latent_query, latent, block_lists, value_up, out_weight
):
    y, z, core, x, w = (lax.axis_index(name) for name in ("y", "z", "c", "x", "w"))
    ctx_pos = (y * NZ + z) * NC + core
    head_pos = x * NW + w

    own = lax.dynamic_slice_in_dim(latent, x * 32, 32, 0).reshape(1, NC, ROWS, LAT)
    wide = jnp.broadcast_to(own, (NY * NZ, NC, ROWS, LAT)).reshape(NBLK, ROWS, LAT)

    key_rows = jnp.moveaxis(index_key.reshape(8, 16, IDX_DIM), 0, 1).reshape(16, 1024)
    packed = jnp.concatenate([key_rows, out_weight.T], axis=0)
    beside = lax.ppermute(packed, "z", [(at, at ^ 1) for at in range(NZ)])
    pair = jnp.stack([packed, beside])
    across = lax.ppermute(pair, "z", [(at, at ^ 2) for at in range(NZ)])
    pool = lax.all_to_all(wide, CTX, 0, 0)
    listed = block_lists[0]
    safe = jnp.maximum(listed, 0)
    both = jnp.concatenate([safe, swap_core(safe)])
    offsets = [
        ((x + step) % NX) * 32 + (core ^ half) * ROWS
        for step in (0, 3, 1, 2)
        for half in range(NC)
    ]
    place = jnp.concatenate([listed, jnp.stack([ctx_pos * BLOCK] + offsets)])
    queries, up_t = prepare(latent_query, value_up)
    near_z = arrange(z.reshape(1), pair, across)
    gathered = lax.all_gather(near_z, "y", axis=0, tiled=True)
    pool, queries, up_t, both, place = lax.optimization_barrier(
        (pool, queries, up_t, both, place)
    )

    picked = jnp.take(pool, both, axis=0, mode="clip").reshape(2, TOPK * ROWS, LAT)
    mine = jnp.concatenate([picked[0], swap_core(picked[1])], axis=0)
    up = [(at, (at + 1) % NX) for at in range(NX)]
    down = [(at, (at - 1) % NX) for at in range(NX)]
    left = lax.ppermute(mine, "x", up)
    right = lax.ppermute(mine, "x", down)

    state = attend(0, place, queries, [mine], None, None)
    left, right, state = lax.optimization_barrier((left, right, state))
    far_a = lax.ppermute(left[:256], "x", up)
    far_b = lax.ppermute(right[256:], "x", down)
    state = attend(2, place, queries, [left, right], state, None)
    far_a, far_b, state = lax.optimization_barrier((far_a, far_b, state))
    values = attend(6, place, queries, [far_a, far_b], state, up_t)

    values, gathered = lax.optimization_barrier((values, gathered))
    terms = project(gathered, values, swap_core(values))
    terms, gathered = lax.optimization_barrier((terms, gathered))
    keys_own = gathered[:, :16]
    keys_other = swap_core(keys_own)
    shares = lax.all_to_all(terms.reshape(NX, NW, NZ * COLS, 2 * BLOCK), "x", 0, 0)
    first_row = ctx_pos * TOK_DEV + head_pos * 16
    index_scores = index_part(
        jnp.stack([core, first_row]), index_query, index_weight, keys_own, keys_other
    )
    shares, index_scores = lax.optimization_barrier((shares, index_scores))
    summed = jnp.sum(shares.astype(jnp.float32), axis=0)
    sent = jnp.where(w == 0, summed[1], summed[0]).astype(jnp.bfloat16)
    kept = jnp.where(w == 0, summed[0], summed[1])
    came = lax.ppermute(sent, "w", [(0, 1), (1, 0)])
    summed = (kept + came.astype(jnp.float32)).astype(jnp.bfloat16)
    kept = summed[:, :BLOCK].reshape(NZ, COLS, BLOCK)
    other = swap_core(summed[:, BLOCK:]).reshape(NZ, COLS, BLOCK)
    first = jnp.where(core == 0, kept, other)
    second = jnp.where(core == 0, other, kept)
    attn_out = jnp.stack([first, second], axis=1).reshape(NZ * NC * COLS, BLOCK).T

    return index_scores, attn_out


def solution(mesh):
    fine = Mesh(mesh.devices.reshape(NY, NZ, NC, NX, NW), ("y", "z", "c", "x", "w"))
    return jax.shard_map(
        body,
        mesh=fine,
        in_specs=(
            P(CTX + HEAD, None),
            P(CTX + HEAD, None),
            P(CTX, None),
            P(CTX, HEAD),
            P(CTX, None),
            P(CTX, None),
            P(HEAD, None, None),
            P(HEAD, CTX),
        ),
        out_specs=(P(CTX + HEAD, None), P(CTX, HEAD)),
        check_vma=False,
    )
```

```python
import functools

import jax
import jax.numpy as jnp
from jax import lax
from jax.experimental import pallas as pl
from jax.experimental.pallas import tpu as pltpu
from jax.sharding import Mesh
from jax.sharding import PartitionSpec as P

TOK_DEV = 128
HEADS_DEV = 8
KV_RANK = 512
LAT = 576
V_DIM = 128
IDX_HEADS = 32
IDX_DIM = 128
BLOCK = 128
TOPK = 16
NBLK = 64
ROWS = 16
PACKED = 72
SHARED = 8
STEPS = 2
COLS = 56
NY, NZ, NC, NX, NW = 8, 4, 2, 4, 2

CTX = ("y", "z", "c")
HEAD = ("x", "w")
LOG2E = 1.4426950408889634
SCORE_SCALE = 192.0 ** (-0.5) * LOG2E
MASKED = -1e30
VMEM_LIMIT = 56 * 1024 * 1024


def attend_kernel(start, count, first, last, *refs):
    place_ref, q_ref = refs[:2]
    kv_refs = refs[2 : 2 + count]
    refs = refs[2 + count :]
    if not first:
        max_in, total_in, sum_in = refs[:3]
        refs = refs[3:]
    if last:
        up_ref, out_ref = refs[:2]
        refs = refs[2:]
    else:
        max_out, total_out, sum_out = refs[:3]
        refs = refs[3:]
    bias_ref, vt_ref = refs[:2]
    waits = []
    if not first:
        held, sem = refs[2], refs[-1]
        waits.append(pltpu.make_async_copy(sum_in, held, sem.at[0]))
        sum_in = held
    if last:
        held_up = refs[3]
        waits.append(pltpu.make_async_copy(up_ref, held_up, sem.at[1]))
        up_ref = held_up
    for copy in waits:
        copy.start()
    keys = jnp.concatenate([ref[...] for ref in kv_refs], axis=0)
    n_keys = keys.shape[0]
    vt_ref[...] = keys[:, :KV_RANK].T
    row = lax.broadcasted_iota(jnp.int32, (ROWS, BLOCK), 0)
    query = place_ref[TOPK] + lax.broadcasted_iota(jnp.int32, (ROWS, BLOCK), 1)
    for group in range(n_keys // ROWS):
        part, slot = divmod(group, TOPK)
        entry = place_ref[slot]
        first_key = jnp.where(entry < 0, 2 * NBLK, entry) * BLOCK
        first_key = first_key + place_ref[TOPK + 1 + start + part]
        seen = jnp.where(first_key + row <= query, 0.0, MASKED)
        bias_ref[group * ROWS : (group + 1) * ROWS, :] = jnp.concatenate([seen] * SHARED, axis=1)
    for pair in range(HEADS_DEV // SHARED):
        scores = lax.dot_general(
            keys, q_ref[pair], (((1,), (1,)), ((), ())), preferred_element_type=jnp.float32
        )
        scores = scores + bias_ref[...]
        row_max = jnp.max(scores, axis=0, keepdims=True)
        if not first:
            row_max = jnp.maximum(row_max, max_in[pair])
            keep = jnp.exp2((max_in[pair] - row_max) * SCORE_SCALE)
        expo = jnp.exp2((scores - row_max) * SCORE_SCALE)
        total = jnp.sum(expo, axis=0, keepdims=True)
        lat_sum = lax.dot_general(
            vt_ref[...],
            expo.astype(jnp.bfloat16),
            (((1,), (0,)), ((), ())),
            preferred_element_type=jnp.float32,
        )
        if pair == 0:
            for copy in waits:
                copy.wait()
        if not first:
            total = total + total_in[pair] * keep
            lat_sum = lat_sum + sum_in[pair] * keep
        if not last:
            max_out[pair] = row_max
            total_out[pair] = total
            sum_out[pair] = lat_sum
            continue
        lat_out = (lat_sum / total).astype(jnp.bfloat16)
        for half in range(SHARED):
            head = SHARED * pair + half
            values = lax.dot_general(
                up_ref[head],
                lat_out[:, half * BLOCK : (half + 1) * BLOCK],
                (((1,), (0,)), ((), ())),
                preferred_element_type=jnp.float32,
            )
            out_ref[head * V_DIM : (head + 1) * V_DIM, :] = values.astype(jnp.bfloat16)


def attend(start, place, queries, parts, state, up_t):
    pairs = HEADS_DEV // SHARED
    n_keys = sum(part.shape[0] for part in parts)
    stat = jax.ShapeDtypeStruct((pairs, 1, SHARED * BLOCK), jnp.float32)
    out = (stat, stat, jax.ShapeDtypeStruct((pairs, KV_RANK, SHARED * BLOCK), jnp.float32))
    last = up_t is not None
    operands = [place, queries, *parts, *(state or ())]
    if last:
        operands.append(up_t)
        out = jax.ShapeDtypeStruct((HEADS_DEV * V_DIM, BLOCK), jnp.bfloat16)
    vmem = pl.BlockSpec(memory_space=pltpu.VMEM)
    outside = pl.BlockSpec(memory_space=pl.ANY)
    specs = [pl.BlockSpec(memory_space=pltpu.SMEM)] + [vmem] * (1 + len(parts))
    scratch = [
        pltpu.VMEM((n_keys, SHARED * BLOCK), jnp.float32),
        pltpu.VMEM((KV_RANK, n_keys), jnp.bfloat16),
    ]
    if state is not None:
        specs += [vmem, vmem, outside]
        scratch.append(pltpu.VMEM((pairs, KV_RANK, SHARED * BLOCK), jnp.float32))
    if last:
        specs.append(outside)
        scratch.append(pltpu.VMEM(up_t.shape, jnp.bfloat16))
    if state is not None:
        scratch.append(pltpu.SemaphoreType.DMA((2,)))
    rows = HEADS_DEV * BLOCK
    return pl.pallas_call(
        functools.partial(attend_kernel, start, len(parts), state is None, last),
        out_shape=out,
        in_specs=specs,
        out_specs=vmem if last else (vmem,) * 3,
        scratch_shapes=scratch,
        compiler_params=pltpu.CompilerParams(vmem_limit_bytes=VMEM_LIMIT),
        cost_estimate=pl.CostEstimate(
            flops=20000000000,
            bytes_accessed=4 * rows * KV_RANK * 2,
            transcendentals=rows * n_keys,
        ),
        name="attend",
    )(*operands)


def index_kernel(place_ref, query_ref, w_ref, own_ref, other_ref, out_ref, wb_ref, q_ref):
    core = place_ref[0]
    first_row = place_ref[1]
    rows = 16
    for head in range(IDX_HEADS):
        q_ref[head * rows : (head + 1) * rows, :] = query_ref[
            :, head * IDX_DIM : (head + 1) * IDX_DIM
        ]
        wb_ref[head * rows : (head + 1) * rows, :] = jnp.broadcast_to(
            w_ref[:, head : head + 1] * (IDX_DIM ** (-0.5)), (rows, BLOCK)
        )
    row_pos = first_row + lax.broadcasted_iota(jnp.int32, (rows, BLOCK), 0)
    lane = lax.broadcasted_iota(jnp.int32, (rows, BLOCK), 1)

    def chunk(keys_ref, parity, step):
        keys = jnp.concatenate(
            [
                keys_ref[step * 2 + half, :, at * IDX_DIM : (at + 1) * IDX_DIM]
                for half in range(2)
                for at in range(8)
            ],
            axis=0,
        )
        dots = lax.dot_general(
            q_ref[...], keys, (((1,), (1,)), ((), ())), preferred_element_type=jnp.float32
        )
        for half in range(2):
            part = dots[:, half * BLOCK : (half + 1) * BLOCK]
            active = jnp.maximum(part, 0.0) * wb_ref[...]
            summed = jnp.sum(active.reshape(IDX_HEADS, rows, BLOCK), axis=0)
            start = pl.multiple_of(((step * 2 + half) * 2 + parity) * BLOCK, BLOCK)
            out_ref[:, pl.ds(start, BLOCK)] = jnp.where(start + lane <= row_pos, summed, 0.0)

    def one(step, carry):
        chunk(own_ref, core, step)
        chunk(other_ref, 1 - core, step)
        return carry

    lax.fori_loop(0, NBLK // 4, one, 0)


def index_part(place, query, weight, own, other):
    return pl.pallas_call(
        index_kernel,
        out_shape=jax.ShapeDtypeStruct((16, NBLK * BLOCK), jnp.float32),
        in_specs=[pl.BlockSpec(memory_space=pltpu.SMEM)]
        + [pl.BlockSpec(memory_space=pltpu.VMEM)] * 4,
        out_specs=pl.BlockSpec(memory_space=pltpu.VMEM),
        scratch_shapes=[
            pltpu.VMEM((IDX_HEADS * 16, BLOCK), jnp.float32),
            pltpu.VMEM((IDX_HEADS * 16, IDX_DIM), jnp.bfloat16),
        ],
        compiler_params=pltpu.CompilerParams(vmem_limit_bytes=VMEM_LIMIT),
        cost_estimate=pl.CostEstimate(
            flops=100_000_000, bytes_accessed=100_000, transcendentals=0
        ),
        name="index_scores",
    )(place, query, weight, own, other)


def prepare_kernel(lq_ref, up_ref, q_ref, up_t_ref):
    for head in range(HEADS_DEV):
        pair, half = divmod(head, SHARED)
        q_ref[pair, half * BLOCK : (half + 1) * BLOCK, :] = lq_ref[:, head * LAT : (head + 1) * LAT]
        up_t_ref[head] = up_ref[head].T


def prepare(latent_query, value_up):
    vmem = pl.BlockSpec(memory_space=pltpu.VMEM)
    shapes = [(HEADS_DEV // SHARED, SHARED * BLOCK, LAT), (HEADS_DEV, V_DIM, KV_RANK)]
    return pl.pallas_call(
        prepare_kernel,
        out_shape=[jax.ShapeDtypeStruct(shape, jnp.bfloat16) for shape in shapes],
        in_specs=[vmem] * 2,
        out_specs=[vmem] * 2,
        compiler_params=pltpu.CompilerParams(vmem_limit_bytes=VMEM_LIMIT),
        cost_estimate=pl.CostEstimate(
            flops=80000000000, bytes_accessed=209715200, transcendentals=0
        ),
        name="prepare",
    )(latent_query, value_up)


def arrange_kernel(z_ref, *refs):
    out_ref = refs[NZ]
    for step in range(NZ):
        out_ref[z_ref[0] ^ step] = refs[step][...]


def arrange(z, near):
    vmem = pl.BlockSpec(memory_space=pltpu.VMEM)
    return pl.pallas_call(
        arrange_kernel,
        out_shape=jax.ShapeDtypeStruct((NZ, PACKED, 1024), jnp.bfloat16),
        in_specs=[pl.BlockSpec(memory_space=pltpu.SMEM)] + [vmem] * NZ,
        out_specs=vmem,
        compiler_params=pltpu.CompilerParams(vmem_limit_bytes=VMEM_LIMIT),
        name="arrange",
    )(z, *near)


def project_kernel(w_ref, own_ref, other_ref, out_ref, values_ref):
    @pl.when(pl.program_id(0) == 0)
    def _():
        values_ref[:, :BLOCK] = own_ref[...]
        values_ref[:, BLOCK:] = other_ref[...]

    terms = lax.dot_general(
        w_ref[...].reshape(NY * NZ * PACKED // STEPS, 1024),
        values_ref[...],
        (((1,), (0,)), ((), ())),
        preferred_element_type=jnp.float32,
    )
    terms = terms.reshape(NY * NZ // STEPS, PACKED, 2 * BLOCK)[:, 16:, :]
    out_ref[...] = terms.reshape(NY // STEPS, NZ * COLS, 2 * BLOCK).astype(jnp.bfloat16)


def project(gathered, own, other):
    values = pl.BlockSpec((HEADS_DEV * V_DIM, BLOCK), lambda i: (0, 0))
    return pl.pallas_call(
        project_kernel,
        out_shape=jax.ShapeDtypeStruct((NY, NZ * COLS, 2 * BLOCK), jnp.bfloat16),
        grid=(STEPS,),
        in_specs=[pl.BlockSpec((NY * NZ // STEPS, PACKED, 1024), lambda i: (i, 0, 0)), values, values],
        out_specs=pl.BlockSpec((NY // STEPS, NZ * COLS, 2 * BLOCK), lambda i: (i, 0, 0)),
        scratch_shapes=[pltpu.VMEM((HEADS_DEV * V_DIM, 2 * BLOCK), jnp.bfloat16)],
        compiler_params=pltpu.CompilerParams(vmem_limit_bytes=VMEM_LIMIT),
        name="project",
    )(gathered, own, other)


def swap_core(value):
    return lax.ppermute(value, "c", [(0, 1), (1, 0)])


def spread(value, axis, count):
    wide = jnp.broadcast_to(value[None], (count,) + value.shape)
    return lax.all_to_all(wide, axis, 0, 0)


def body(
    index_query, index_weight, index_key, latent_query, latent, block_lists, value_up, out_weight
):
    y, z, core, x, w = (lax.axis_index(name) for name in ("y", "z", "c", "x", "w"))
    ctx_pos = (y * NZ + z) * NC + core
    head_pos = x * NW + w

    own = lax.dynamic_slice_in_dim(latent, x * 32, 32, 0).reshape(1, NC, ROWS, LAT)
    wide = jnp.broadcast_to(own, (NY * NZ, NC, ROWS, LAT)).reshape(NBLK, ROWS, LAT)

    key_rows = jnp.moveaxis(index_key.reshape(8, 16, IDX_DIM), 0, 1).reshape(16, 1024)
    packed = jnp.concatenate([key_rows, out_weight.T], axis=0)
    near = [packed] + [
        lax.ppermute(packed, "z", [(at, at ^ step) for at in range(NZ)]) for step in range(1, NZ)
    ]
    pool = lax.all_to_all(wide, CTX, 0, 0)
    listed = block_lists[0]
    safe = jnp.maximum(listed, 0)
    both = jnp.concatenate([safe, swap_core(safe)])
    offsets = [
        ((x + step) % NX) * 32 + (core ^ half) * ROWS
        for step in (0, 3, 1, 2)
        for half in range(NC)
    ]
    place = jnp.concatenate([listed, jnp.stack([ctx_pos * BLOCK] + offsets)])
    queries, up_t = prepare(latent_query, value_up)
    near_z = arrange(z.reshape(1), near)
    gathered = lax.all_gather(near_z, "y", axis=0, tiled=True)
    pool, queries, up_t, both, place = lax.optimization_barrier(
        (pool, queries, up_t, both, place)
    )

    picked = jnp.take(pool, both, axis=0, mode="clip").reshape(2, TOPK * ROWS, LAT)
    mine = jnp.concatenate([picked[0], swap_core(picked[1])], axis=0)
    up = [(at, (at + 1) % NX) for at in range(NX)]
    down = [(at, (at - 1) % NX) for at in range(NX)]
    left = lax.ppermute(mine, "x", up)
    right = lax.ppermute(mine, "x", down)

    state = attend(0, place, queries, [mine], None, None)
    left, right, state = lax.optimization_barrier((left, right, state))
    far_a = lax.ppermute(left[:256], "x", up)
    far_b = lax.ppermute(right[256:], "x", down)
    state = attend(2, place, queries, [left, right], state, None)
    far_a, far_b, state = lax.optimization_barrier((far_a, far_b, state))
    values = attend(6, place, queries, [far_a, far_b], state, up_t)

    values, gathered = lax.optimization_barrier((values, gathered))
    terms = project(gathered, values, swap_core(values))
    terms, gathered = lax.optimization_barrier((terms, gathered))
    keys_own = gathered[:, :16]
    keys_other = swap_core(keys_own)
    shares = lax.all_to_all(terms.reshape(NX, NW, NZ * COLS, 2 * BLOCK), "x", 0, 0)
    first_row = ctx_pos * TOK_DEV + head_pos * 16
    index_scores = index_part(
        jnp.stack([core, first_row]), index_query, index_weight, keys_own, keys_other
    )
    shares, index_scores = lax.optimization_barrier((shares, index_scores))
    summed = jnp.sum(shares.astype(jnp.float32), axis=0)
    sent = jnp.where(w == 0, summed[1], summed[0]).astype(jnp.bfloat16)
    kept = jnp.where(w == 0, summed[0], summed[1])
    came = lax.ppermute(sent, "w", [(0, 1), (1, 0)])
    summed = (kept + came.astype(jnp.float32)).astype(jnp.bfloat16)
    kept = summed[:, :BLOCK].reshape(NZ, COLS, BLOCK)
    other = swap_core(summed[:, BLOCK:]).reshape(NZ, COLS, BLOCK)
    first = jnp.where(core == 0, kept, other)
    second = jnp.where(core == 0, other, kept)
    attn_out = jnp.stack([first, second], axis=1).reshape(NZ * NC * COLS, BLOCK).T

    return index_scores, attn_out


def solution(mesh):
    fine = Mesh(mesh.devices.reshape(NY, NZ, NC, NX, NW), ("y", "z", "c", "x", "w"))
    return jax.shard_map(
        body,
        mesh=fine,
        in_specs=(
            P(CTX + HEAD, None),
            P(CTX + HEAD, None),
            P(CTX, None),
            P(CTX, HEAD),
            P(CTX, None),
            P(CTX, None),
            P(HEAD, None, None),
            P(HEAD, CTX),
        ),
        out_specs=(P(CTX + HEAD, None), P(CTX, HEAD)),
        check_vma=False,
    )
```

```python
import functools

import jax
import jax.numpy as jnp
from jax import lax
from jax.experimental import pallas as pl
from jax.experimental.pallas import tpu as pltpu
from jax.sharding import Mesh
from jax.sharding import PartitionSpec as P

TOK_DEV = 128
HEADS_DEV = 8
KV_RANK = 512
LAT = 576
V_DIM = 128
IDX_HEADS = 32
IDX_DIM = 128
BLOCK = 128
TOPK = 16
NBLK = 64
ROWS = 16
PACKED = 72
SHARED = 8
STEPS = 2
COLS = 56
NY, NZ, NC, NX, NW = 8, 4, 2, 4, 2

CTX = ("y", "z", "c")
HEAD = ("x", "w")
LOG2E = 1.4426950408889634
SCORE_SCALE = 192.0 ** (-0.5) * LOG2E
MASKED = -1e30
VMEM_LIMIT = 56 * 1024 * 1024


def attend_kernel(start, count, first, last, *refs):
    place_ref, q_ref = refs[:2]
    kv_refs = refs[2 : 2 + count]
    refs = refs[2 + count :]
    if not first:
        max_in, total_in, sum_in = refs[:3]
        refs = refs[3:]
    if last:
        up_ref, out_ref = refs[:2]
        refs = refs[2:]
    else:
        max_out, total_out, sum_out = refs[:3]
        refs = refs[3:]
    bias_ref, vt_ref = refs[:2]
    waits = []
    if not first and not last:
        held, sem = refs[2], refs[-1]
        waits.append(pltpu.make_async_copy(sum_in, held, sem))
        sum_in = held
    for copy in waits:
        copy.start()
    keys = jnp.concatenate([ref[...] for ref in kv_refs], axis=0)
    n_keys = keys.shape[0]
    vt_ref[...] = keys[:, :KV_RANK].T
    row = lax.broadcasted_iota(jnp.int32, (ROWS, BLOCK), 0)
    query = place_ref[TOPK] + lax.broadcasted_iota(jnp.int32, (ROWS, BLOCK), 1)
    for group in range(n_keys // ROWS):
        part, slot = divmod(group, TOPK)
        entry = place_ref[slot]
        first_key = jnp.where(entry < 0, 2 * NBLK, entry) * BLOCK
        first_key = first_key + place_ref[TOPK + 1 + start + part]
        seen = jnp.where(first_key + row <= query, 0.0, MASKED)
        bias_ref[group * ROWS : (group + 1) * ROWS, :] = jnp.concatenate([seen] * SHARED, axis=1)
    for pair in range(HEADS_DEV // SHARED):
        scores = lax.dot_general(
            keys, q_ref[pair], (((1,), (1,)), ((), ())), preferred_element_type=jnp.float32
        )
        scores = scores + bias_ref[...]
        row_max = jnp.max(scores, axis=0, keepdims=True)
        if not first:
            row_max = jnp.maximum(row_max, max_in[pair])
            keep = jnp.exp2((max_in[pair] - row_max) * SCORE_SCALE)
        expo = jnp.exp2((scores - row_max) * SCORE_SCALE)
        total = jnp.sum(expo, axis=0, keepdims=True)
        lat_sum = lax.dot_general(
            vt_ref[...],
            expo.astype(jnp.bfloat16),
            (((1,), (0,)), ((), ())),
            preferred_element_type=jnp.float32,
        )
        if pair == 0:
            for copy in waits:
                copy.wait()
        if not first:
            total = total + total_in[pair] * keep
            lat_sum = lat_sum + sum_in[pair] * keep
        if not last:
            max_out[pair] = row_max
            total_out[pair] = total
            sum_out[pair] = lat_sum
            continue
        lat_out = (lat_sum / total).astype(jnp.bfloat16)
        for half in range(SHARED):
            head = SHARED * pair + half
            values = lax.dot_general(
                up_ref[head],
                lat_out[:, half * BLOCK : (half + 1) * BLOCK],
                (((1,), (0,)), ((), ())),
                preferred_element_type=jnp.float32,
            )
            out_ref[head * V_DIM : (head + 1) * V_DIM, :] = values.astype(jnp.bfloat16)


def attend(start, place, queries, parts, state, up_t):
    pairs = HEADS_DEV // SHARED
    n_keys = sum(part.shape[0] for part in parts)
    stat = jax.ShapeDtypeStruct((pairs, 1, SHARED * BLOCK), jnp.float32)
    out = (stat, stat, jax.ShapeDtypeStruct((pairs, KV_RANK, SHARED * BLOCK), jnp.float32))
    last = up_t is not None
    operands = [place, queries, *parts, *(state or ())]
    if last:
        operands.append(up_t)
        out = jax.ShapeDtypeStruct((HEADS_DEV * V_DIM, BLOCK), jnp.bfloat16)
    vmem = pl.BlockSpec(memory_space=pltpu.VMEM)
    outside = pl.BlockSpec(memory_space=pl.ANY)
    specs = [pl.BlockSpec(memory_space=pltpu.SMEM)] + [vmem] * (1 + len(parts))
    scratch = [
        pltpu.VMEM((n_keys, SHARED * BLOCK), jnp.float32),
        pltpu.VMEM((KV_RANK, n_keys), jnp.bfloat16),
    ]
    if state is not None:
        specs += [vmem, vmem, vmem if last else outside]
    if last:
        specs.append(vmem)
    elif state is not None:
        scratch.append(pltpu.VMEM((pairs, KV_RANK, SHARED * BLOCK), jnp.float32))
        scratch.append(pltpu.SemaphoreType.DMA)
    rows = HEADS_DEV * BLOCK
    return pl.pallas_call(
        functools.partial(attend_kernel, start, len(parts), state is None, last),
        out_shape=out,
        in_specs=specs,
        out_specs=vmem if last else (vmem,) * 3,
        scratch_shapes=scratch,
        compiler_params=pltpu.CompilerParams(vmem_limit_bytes=VMEM_LIMIT),
        cost_estimate=pl.CostEstimate(
            flops=20000000000,
            bytes_accessed=4 * rows * KV_RANK * 2,
            transcendentals=rows * n_keys,
        ),
        name="attend",
    )(*operands)


def index_kernel(place_ref, query_ref, w_ref, own_ref, other_ref, out_ref, wb_ref, q_ref):
    core = place_ref[0]
    first_row = place_ref[1]
    rows = 16
    for head in range(IDX_HEADS):
        q_ref[head * rows : (head + 1) * rows, :] = query_ref[
            :, head * IDX_DIM : (head + 1) * IDX_DIM
        ]
        wb_ref[head * rows : (head + 1) * rows, :] = jnp.broadcast_to(
            w_ref[:, head : head + 1] * (IDX_DIM ** (-0.5)), (rows, BLOCK)
        )
    row_pos = first_row + lax.broadcasted_iota(jnp.int32, (rows, BLOCK), 0)
    lane = lax.broadcasted_iota(jnp.int32, (rows, BLOCK), 1)

    def chunk(keys_ref, parity, step):
        keys = jnp.concatenate(
            [
                keys_ref[step * 2 + half, :, at * IDX_DIM : (at + 1) * IDX_DIM]
                for half in range(2)
                for at in range(8)
            ],
            axis=0,
        )
        dots = lax.dot_general(
            q_ref[...], keys, (((1,), (1,)), ((), ())), preferred_element_type=jnp.float32
        )
        for half in range(2):
            part = dots[:, half * BLOCK : (half + 1) * BLOCK]
            active = jnp.maximum(part, 0.0) * wb_ref[...]
            summed = jnp.sum(active.reshape(IDX_HEADS, rows, BLOCK), axis=0)
            start = pl.multiple_of(((step * 2 + half) * 2 + parity) * BLOCK, BLOCK)
            out_ref[:, pl.ds(start, BLOCK)] = jnp.where(start + lane <= row_pos, summed, 0.0)

    def one(step, carry):
        chunk(own_ref, core, step)
        chunk(other_ref, 1 - core, step)
        return carry

    lax.fori_loop(0, NBLK // 4, one, 0)


def index_part(place, query, weight, own, other):
    return pl.pallas_call(
        index_kernel,
        out_shape=jax.ShapeDtypeStruct((16, NBLK * BLOCK), jnp.float32),
        in_specs=[pl.BlockSpec(memory_space=pltpu.SMEM)]
        + [pl.BlockSpec(memory_space=pltpu.VMEM)] * 4,
        out_specs=pl.BlockSpec(memory_space=pltpu.VMEM),
        scratch_shapes=[
            pltpu.VMEM((IDX_HEADS * 16, BLOCK), jnp.float32),
            pltpu.VMEM((IDX_HEADS * 16, IDX_DIM), jnp.bfloat16),
        ],
        compiler_params=pltpu.CompilerParams(vmem_limit_bytes=VMEM_LIMIT),
        cost_estimate=pl.CostEstimate(
            flops=100_000_000, bytes_accessed=100_000, transcendentals=0
        ),
        name="index_scores",
    )(place, query, weight, own, other)


def prepare_kernel(lq_ref, up_ref, q_ref, up_t_ref):
    for head in range(HEADS_DEV):
        pair, half = divmod(head, SHARED)
        q_ref[pair, half * BLOCK : (half + 1) * BLOCK, :] = lq_ref[:, head * LAT : (head + 1) * LAT]
        up_t_ref[head] = up_ref[head].T


def prepare(latent_query, value_up):
    vmem = pl.BlockSpec(memory_space=pltpu.VMEM)
    shapes = [(HEADS_DEV // SHARED, SHARED * BLOCK, LAT), (HEADS_DEV, V_DIM, KV_RANK)]
    return pl.pallas_call(
        prepare_kernel,
        out_shape=[jax.ShapeDtypeStruct(shape, jnp.bfloat16) for shape in shapes],
        in_specs=[vmem] * 2,
        out_specs=[vmem] * 2,
        compiler_params=pltpu.CompilerParams(vmem_limit_bytes=VMEM_LIMIT),
        cost_estimate=pl.CostEstimate(
            flops=80000000000, bytes_accessed=209715200, transcendentals=0
        ),
        name="prepare",
    )(latent_query, value_up)


def arrange_kernel(z_ref, *refs):
    out_ref = refs[NZ]
    for step in range(NZ):
        out_ref[z_ref[0] ^ step] = refs[step][...]


def arrange(z, near):
    vmem = pl.BlockSpec(memory_space=pltpu.VMEM)
    return pl.pallas_call(
        arrange_kernel,
        out_shape=jax.ShapeDtypeStruct((NZ, PACKED, 1024), jnp.bfloat16),
        in_specs=[pl.BlockSpec(memory_space=pltpu.SMEM)] + [vmem] * NZ,
        out_specs=vmem,
        compiler_params=pltpu.CompilerParams(vmem_limit_bytes=VMEM_LIMIT),
        name="arrange",
    )(z, *near)


def project_kernel(w_ref, own_ref, other_ref, out_ref, values_ref):
    @pl.when(pl.program_id(0) == 0)
    def _():
        values_ref[:, :BLOCK] = own_ref[...]
        values_ref[:, BLOCK:] = other_ref[...]

    terms = lax.dot_general(
        w_ref[...].reshape(NY * NZ * PACKED // STEPS, 1024),
        values_ref[...],
        (((1,), (0,)), ((), ())),
        preferred_element_type=jnp.float32,
    )
    terms = terms.reshape(NY * NZ // STEPS, PACKED, 2 * BLOCK)[:, 16:, :]
    out_ref[...] = terms.reshape(NY // STEPS, NZ * COLS, 2 * BLOCK).astype(jnp.bfloat16)


def project(gathered, own, other):
    values = pl.BlockSpec((HEADS_DEV * V_DIM, BLOCK), lambda i: (0, 0))
    return pl.pallas_call(
        project_kernel,
        out_shape=jax.ShapeDtypeStruct((NY, NZ * COLS, 2 * BLOCK), jnp.bfloat16),
        grid=(STEPS,),
        in_specs=[pl.BlockSpec((NY * NZ // STEPS, PACKED, 1024), lambda i: (i, 0, 0)), values, values],
        out_specs=pl.BlockSpec((NY // STEPS, NZ * COLS, 2 * BLOCK), lambda i: (i, 0, 0)),
        scratch_shapes=[pltpu.VMEM((HEADS_DEV * V_DIM, 2 * BLOCK), jnp.bfloat16)],
        compiler_params=pltpu.CompilerParams(vmem_limit_bytes=VMEM_LIMIT),
        name="project",
    )(gathered, own, other)


def swap_core(value):
    return lax.ppermute(value, "c", [(0, 1), (1, 0)])


def spread(value, axis, count):
    wide = jnp.broadcast_to(value[None], (count,) + value.shape)
    return lax.all_to_all(wide, axis, 0, 0)


def body(
    index_query, index_weight, index_key, latent_query, latent, block_lists, value_up, out_weight
):
    y, z, core, x, w = (lax.axis_index(name) for name in ("y", "z", "c", "x", "w"))
    ctx_pos = (y * NZ + z) * NC + core
    head_pos = x * NW + w

    own = lax.dynamic_slice_in_dim(latent, x * 32, 32, 0).reshape(1, NC, ROWS, LAT)
    wide = jnp.broadcast_to(own, (NY * NZ, NC, ROWS, LAT)).reshape(NBLK, ROWS, LAT)

    key_rows = jnp.moveaxis(index_key.reshape(8, 16, IDX_DIM), 0, 1).reshape(16, 1024)
    packed = jnp.concatenate([key_rows, out_weight.T], axis=0)
    near = [packed] + [
        lax.ppermute(packed, "z", [(at, at ^ step) for at in range(NZ)]) for step in range(1, NZ)
    ]
    pool = lax.all_to_all(wide, CTX, 0, 0)
    listed = block_lists[0]
    safe = jnp.maximum(listed, 0)
    both = jnp.concatenate([safe, swap_core(safe)])
    offsets = [
        ((x + step) % NX) * 32 + (core ^ half) * ROWS
        for step in (0, 3, 1, 2)
        for half in range(NC)
    ]
    place = jnp.concatenate([listed, jnp.stack([ctx_pos * BLOCK] + offsets)])
    queries, up_t = prepare(latent_query, value_up)
    near_z = arrange(z.reshape(1), near)
    gathered = lax.all_gather(near_z, "y", axis=0, tiled=True)
    pool, queries, up_t, both, place = lax.optimization_barrier(
        (pool, queries, up_t, both, place)
    )

    picked = jnp.take(pool, both, axis=0, mode="clip").reshape(2, TOPK * ROWS, LAT)
    mine = jnp.concatenate([picked[0], swap_core(picked[1])], axis=0)
    up = [(at, (at + 1) % NX) for at in range(NX)]
    down = [(at, (at - 1) % NX) for at in range(NX)]
    left = lax.ppermute(mine, "x", up)
    right = lax.ppermute(mine, "x", down)

    state = attend(0, place, queries, [mine], None, None)
    left, right, state = lax.optimization_barrier((left, right, state))
    far_a = lax.ppermute(left[:256], "x", up)
    far_b = lax.ppermute(right[256:], "x", down)
    state = attend(2, place, queries, [left, right], state, None)
    far_a, far_b, state = lax.optimization_barrier((far_a, far_b, state))
    values = attend(6, place, queries, [far_a, far_b], state, up_t)

    values, gathered = lax.optimization_barrier((values, gathered))
    terms = project(gathered, values, swap_core(values))
    terms, gathered = lax.optimization_barrier((terms, gathered))
    keys_own = gathered[:, :16]
    keys_other = swap_core(keys_own)
    shares = lax.all_to_all(terms.reshape(NX, NW, NZ * COLS, 2 * BLOCK), "x", 0, 0)
    first_row = ctx_pos * TOK_DEV + head_pos * 16
    index_scores = index_part(
        jnp.stack([core, first_row]), index_query, index_weight, keys_own, keys_other
    )
    shares, index_scores = lax.optimization_barrier((shares, index_scores))
    summed = jnp.sum(shares.astype(jnp.float32), axis=0)
    sent = jnp.where(w == 0, summed[1], summed[0]).astype(jnp.bfloat16)
    kept = jnp.where(w == 0, summed[0], summed[1])
    came = lax.ppermute(sent, "w", [(0, 1), (1, 0)])
    summed = (kept + came.astype(jnp.float32)).astype(jnp.bfloat16)
    kept = summed[:, :BLOCK].reshape(NZ, COLS, BLOCK)
    other = swap_core(summed[:, BLOCK:]).reshape(NZ, COLS, BLOCK)
    first = jnp.where(core == 0, kept, other)
    second = jnp.where(core == 0, other, kept)
    attn_out = jnp.stack([first, second], axis=1).reshape(NZ * NC * COLS, BLOCK).T

    return index_scores, attn_out


def solution(mesh):
    fine = Mesh(mesh.devices.reshape(NY, NZ, NC, NX, NW), ("y", "z", "c", "x", "w"))
    return jax.shard_map(
        body,
        mesh=fine,
        in_specs=(
            P(CTX + HEAD, None),
            P(CTX + HEAD, None),
            P(CTX, None),
            P(CTX, HEAD),
            P(CTX, None),
            P(CTX, None),
            P(HEAD, None, None),
            P(HEAD, CTX),
        ),
        out_specs=(P(CTX + HEAD, None), P(CTX, HEAD)),
        check_vma=False,
    )
```
